512 devices in a mesh: rep: 8 (over y, x_lo), fsdp: 64 (over x_hi, z, core).
Axes of the slice: x: 4 (x_hi: 2, x_lo: 2; x = x_hi * 2 + x_lo), y: 4, z: 16, core: 2. Of those that a mesh axis runs over, the one named last changes fastest.
Arguments:
- x_in: bfloat16 [8, 8192, 512], P('rep', 'fsdp'), may hold values from -16 to 16
- d_out: bfloat16 [8, 8192, 512], P('rep', 'fsdp'), may hold values from -0.375 to 0.375
- gate_weight: bfloat16 [64, 128, 128], P('fsdp'), may hold values from -0.25 to 0.25
- up_weight: bfloat16 [64, 128, 128], P('fsdp'), may hold values from -0.25 to 0.25
- down_weight: bfloat16 [64, 128, 128], P('fsdp'), may hold values from -0.125 to 0.125
- mom_gate: float32 [8, 64, 128, 128], P('rep', 'fsdp'), may hold values from -6 to 6
- mom_up: float32 [8, 64, 128, 128], P('rep', 'fsdp'), may hold values from -6 to 6
- mom_down: float32 [8, 64, 128, 128], P('rep', 'fsdp'), may hold values from -6 to 6
- band_index: int32 [3, 64, 512], P(None, 'fsdp'), may hold values from 0 to 16383, as said below
Outputs:
- res_gate: float32 [8, 64, 128, 128], P('rep', 'fsdp')
- res_up: float32 [8, 64, 128, 128], P('rep', 'fsdp')
- down_residual_blocks: float32 [8, 64, 128, 128], P('rep', 'fsdp')
- upd_gate: float32 [64, 128, 128], P('fsdp')
- upd_up: float32 [64, 128, 128], P('fsdp')
- upd_down: float32 [64, 128, 128], P('fsdp')
The draws below stay inside these ranges and needn't reach their ends.
Inputs may be any that keep to these rules, and one draw needn't show every extreme that they name: `band_index`: each row of 512 positions of a block holds distinct values; the positions are the same for every replica group.
All inputs are finite; a program needn't handle non-finite values.
Results may differ from the reference program's by a relative error of at most 0.0028.
Values may be sent and summed in bfloat16 or wider, within the bound.
A program may use at most 128 MiB of HBM per device.

```python
import jax
import jax.numpy as jnp
from jax import lax

D = 512
FF = 2048
SPAN = 128
K = 512
TOKENS = 8192
MATRIX_PARTS = 64
N_REP = 8


def draw_band_index(key, part):
    key = jax.random.fold_in(key, 11)
    row_keys = jax.random.split(key, 3 * MATRIX_PARTS)

    def one_row(row_key):
        return jax.random.permutation(row_key, SPAN * SPAN)[:K]
    chosen = jax.vmap(one_row)(row_keys)
    return chosen.reshape(3, MATRIX_PARTS, K).astype(jnp.int32)


def strengthened(drawn, stream_key, source, target, blocks, factor):
    owner, partner = [(jnp.arange(drawn.shape[position]) // (drawn.shape[position] // blocks)).reshape([-1 if axis == position else 1 for axis in range(drawn.ndim)]) for position in (source, target)]
    chosen = jax.random.permutation(stream_key, blocks)[partner]
    strong = (owner == chosen) | (owner == (partner + blocks // 2) % blocks)
    return jnp.where(strong, factor * drawn, drawn)


def levels(own_key, extent, pieces, low, largest):
    def one(dim, shards_of):
        heights = jax.random.uniform(jax.random.fold_in(jax.random.fold_in(own_key, 6), dim), (shards_of,), jnp.float32, low / len(pieces), largest / len(pieces))
        return jnp.repeat(jnp.exp(heights), extent[dim] // shards_of).reshape((-1,) + (1,) * (len(extent) - dim - 1))

    gain = one(*pieces[0])
    for cut in pieces[1:]:
        gain = gain * one(*cut)
    return gain


def scatter_about(key, extent, width, most, cuts=(), held_as=jnp.bfloat16):
    values = width * jax.random.normal(key, extent, jnp.float32)
    if cuts:
        values = values * levels(key, extent, cuts, -0.22, 0.18)
    return jnp.clip(values, -most, most).astype(held_as)


def noise_with(own_key, dims, deviation, bound, cuts, heavy, kind=jnp.bfloat16):
    drawn = deviation * jax.random.normal(own_key, dims, jnp.float32)
    if cuts:
        drawn = drawn * levels(own_key, dims, cuts, -0.22, 0.18)
    return jnp.clip(strengthened(drawn, jax.random.fold_in(own_key, 3), *heavy), -bound, bound).astype(kind)


def setup_inputs(seed: int = 0) -> dict:
    streams_of = jax.random.split(jax.random.key(seed), 10)
    x_in = noise_with(streams_of[0], (N_REP, TOKENS, D), 1.0, 16.0, ((0, 8), (1, 64)), (1, 2, 64, 4.0))
    d_out = noise_with(streams_of[1], (N_REP, TOKENS, D), ((FF / (D * TOKENS)) ** 0.5), 0.375, ((0, 8), (1, 64)), (1, 2, 64, 4.0))
    gate_weight = scatter_about(streams_of[2], (MATRIX_PARTS, SPAN, SPAN), D ** -0.5, 0.25, ((0, 64),))
    up_weight = scatter_about(streams_of[3], (MATRIX_PARTS, SPAN, SPAN), D ** -0.5, 0.25, ((0, 64),))
    down_weight = scatter_about(streams_of[4], (MATRIX_PARTS, SPAN, SPAN), FF ** -0.5, 0.125, ((0, 64),))
    mom_gate = scatter_about(streams_of[5], (N_REP, MATRIX_PARTS, SPAN, SPAN), 1.0, 6.0, ((0, 8), (1, 64)), jnp.float32)
    mom_up = scatter_about(streams_of[6], (N_REP, MATRIX_PARTS, SPAN, SPAN), 1.0, 6.0, ((0, 8), (1, 64)), jnp.float32)
    mom_down = scatter_about(streams_of[7], (N_REP, MATRIX_PARTS, SPAN, SPAN), 1.0, 6.0, ((0, 8), (1, 64)), jnp.float32)
    band_index = draw_band_index(jax.random.fold_in(streams_of[9], 71), 0)
    return {"x_in": x_in, "d_out": d_out, "gate_weight": gate_weight, "up_weight": up_weight, "down_weight": down_weight, "mom_gate": mom_gate, "mom_up": mom_up, "mom_down": mom_down, "band_index": band_index}


momentum_decay = 0.999

def dct_table(side_len):
    freq_rows = jnp.arange(side_len, dtype=jnp.float32)[:, None]
    cell_cols = jnp.arange(side_len, dtype=jnp.float32)[None, :]
    weights = jnp.where(freq_rows == 0, jnp.sqrt(1.0 / side_len), jnp.sqrt(2.0 / side_len))
    return weights * jnp.cos(jnp.pi * (2.0 * cell_cols + 1.0) * freq_rows / (2.0 * side_len))

def forward_blocks(cosines, blocks):
    inner = jnp.matmul(cosines, blocks, precision=lax.Precision.HIGHEST)
    return jnp.matmul(inner, cosines.T, precision=lax.Precision.HIGHEST)

def inverse_blocks(cosines, coeffs):
    inner = jnp.matmul(cosines.T, coeffs, precision=lax.Precision.HIGHEST)
    return jnp.matmul(inner, cosines, precision=lax.Precision.HIGHEST)

def place_band(values, positions, side_len):
    layout = (positions.shape[0], positions.shape[1], side_len * side_len)
    matrix_ids = jnp.arange(layout[0])[:, None, None]
    span_ids = jnp.arange(layout[1])[None, :, None]
    filled = jnp.zeros(layout, values.dtype).at[matrix_ids, span_ids, positions].set(values)
    return filled.reshape(layout[0], layout[1], side_len, side_len)

def band_split(moments, gradients, band_index):
    side_len = moments.shape[2]
    updated = momentum_decay * moments + gradients
    cosines = dct_table(side_len)
    coeffs = forward_blocks(cosines, updated)
    flattened = coeffs.reshape(coeffs.shape[0], coeffs.shape[1], side_len * side_len)
    picked = jnp.take_along_axis(flattened, band_index, axis=2)
    kept_part = inverse_blocks(cosines, place_band(picked, band_index, side_len))
    return (updated - kept_part, picked)

def decode_band(summed, band_index, side_len):
    cosines = dct_table(side_len)
    return inverse_blocks(cosines, place_band(summed, band_index, side_len))

def input_full(blocks, row_blocks, col_blocks):
    side_len = blocks.shape[1]
    grid = blocks.reshape(col_blocks, row_blocks, side_len, side_len)
    return grid.transpose(1, 2, 0, 3).reshape(row_blocks * side_len, col_blocks * side_len)

def output_full(blocks, row_blocks, col_blocks):
    side_len = blocks.shape[1]
    grid = blocks.reshape(col_blocks, row_blocks, side_len, side_len)
    return grid.transpose(0, 2, 1, 3).reshape(col_blocks * side_len, row_blocks * side_len)

def input_blocks(matrix, side_len):
    row_blocks = matrix.shape[0] // side_len
    col_blocks = matrix.shape[1] // side_len
    grid = matrix.reshape(row_blocks, side_len, col_blocks, side_len).transpose(2, 0, 1, 3)
    return grid.reshape(row_blocks * col_blocks, side_len, side_len)

def output_blocks(matrix, side_len):
    col_blocks = matrix.shape[0] // side_len
    row_blocks = matrix.shape[1] // side_len
    grid = matrix.reshape(col_blocks, side_len, row_blocks, side_len).transpose(0, 2, 1, 3)
    return grid.reshape(row_blocks * col_blocks, side_len, side_len)

def reference(x_in, d_out, gate_weight, up_weight, down_weight, mom_gate, mom_up, mom_down, band_index):
    side_len = gate_weight.shape[1]
    row_blocks = x_in.shape[2] // side_len
    col_blocks = gate_weight.shape[0] // row_blocks
    gate_whole = input_full(gate_weight, row_blocks, col_blocks)
    up_whole = input_full(up_weight, row_blocks, col_blocks)
    down_whole = output_full(down_weight, row_blocks, col_blocks)

    def per_group(group_items):
        x_rows, d_rows, moment_gate, up_momentum, moment_down = group_items
        gate_pre = jnp.dot(x_rows, gate_whole, preferred_element_type=jnp.float32)
        up_pre = jnp.dot(x_rows, up_whole, preferred_element_type=jnp.float32)
        d_hidden = jnp.dot(d_rows, down_whole.T, preferred_element_type=jnp.float32)
        sigmoid_gate = jax.nn.sigmoid(gate_pre)
        hidden = (gate_pre * sigmoid_gate * up_pre).astype(jnp.bfloat16)
        d_gate = (d_hidden * up_pre * sigmoid_gate * (1.0 + gate_pre * (1.0 - sigmoid_gate))).astype(jnp.bfloat16)
        d_up = (d_hidden * gate_pre * sigmoid_gate).astype(jnp.bfloat16)
        grad_gate = jnp.dot(x_rows.T, d_gate, preferred_element_type=jnp.float32)
        grad_up = jnp.dot(x_rows.T, d_up, preferred_element_type=jnp.float32)
        grad_down = jnp.dot(hidden.T, d_rows, preferred_element_type=jnp.float32)
        gradients = jnp.stack([input_blocks(grad_gate, side_len), input_blocks(grad_up, side_len), output_blocks(grad_down, side_len)])
        moments = jnp.stack([moment_gate, up_momentum, moment_down])
        return band_split(moments, gradients, band_index)
    remains, picked = lax.map(per_group, (x_in, d_out, mom_gate, mom_up, mom_down))
    summed = lax.optimization_barrier(jnp.sum(picked, axis=0))
    updates = decode_band(summed, band_index, side_len)
    return (remains[:, 0], remains[:, 1], remains[:, 2], updates[0], updates[1], updates[2])
```

```python
import functools

import jax
import jax.numpy as jnp
import numpy as np
from jax import lax
from jax.experimental import pallas as pl
from jax.experimental.pallas import tpu as pltpu
from jax.sharding import PartitionSpec as P

MESH = pl.DeviceIdType.MESH
F32 = jnp.float32
BF16 = jnp.bfloat16
SIDE = 128
KEEP = 512
NZ = 16
QROWS = SIDE + 16


def dct_parts():
    k = np.arange(SIDE, dtype=np.float64)[:, None]
    n = np.arange(SIDE, dtype=np.float64)[None, :]
    s = np.where(k == 0, np.sqrt(1.0 / SIDE), np.sqrt(2.0 / SIDE))
    c = (s * np.cos(np.pi * (2.0 * n + 1.0) * k / (2.0 * SIDE))).astype(np.float32)
    out = []
    for t in (c, c.T):
        hi = t.astype(jnp.bfloat16)
        lo = (t - hi.astype(np.float32)).astype(jnp.bfloat16)
        out += [hi, lo]
    return np.stack(out)


def mm(a, b, dims):
    return lax.dot_general(a, b, (dims, ((), ())), preferred_element_type=F32)


NN = ((1,), (0,))
NT = ((1,), (1,))
TN = ((0,), (0,))


def split(a):
    hi = a.astype(BF16)
    return hi, (a - hi.astype(F32)).astype(BF16)


def mm3(a, b, dims):
    return mm(a[0], b[0], dims) + (mm(a[0], b[1], dims) + mm(a[1], b[0], dims))


def quantize(value, dst):
    top = jnp.maximum(jnp.max(jnp.abs(value), axis=0, keepdims=True), 1e-30)
    power = jnp.ceil(jnp.log2(top))
    steps = jnp.round(value * jnp.exp2(14.0 - power))
    dst[0:SIDE, :] = steps.astype(jnp.int32).astype(jnp.int16)
    dst[SIDE:QROWS, :] = jnp.broadcast_to(power.astype(jnp.int32), (16, SIDE)).astype(jnp.int16)


def restore(src):
    steps = src[0:SIDE, :].astype(jnp.int32).astype(F32)
    power = src[SIDE:QROWS, :].astype(jnp.int32).astype(F32)[0:1, :]
    return steps * jnp.exp2(power - 14.0)


def kernel(
    x_ref, d_ref, wg_ref, wu_ref, wd_ref, mg_ref, mu_ref, md_ref, band_ref, table_ref,
    rg_out, ru_out, rd_out, ug_out, uu_out, ud_out,
    tok_x, tok_d, wts, part, recv, send, fin, own, mom, band, table, pick_r, pick_c, vals, vals_all,
    load_sem, tok_send, tok_recv, sib_sem, ag_send, ag_recv, rs_send, rs_recv, fin_recv, own_sem,
    rep_send, rep_recv,
):
    f = lax.axis_index("fsdp")
    r = lax.axis_index("rep")
    core = f % 2
    z = (f // 2) % NZ
    xh = f // (2 * NZ)
    kz = z // 2
    sib = f + 1 - 2 * core
    partner = (1 - xh) * (2 * NZ) + z * 2 + core
    up = (z + 1) % NZ
    down = (z + NZ - 1) % NZ
    base = xh * (2 * NZ)
    up_same = base + up * 2 + core
    down_same = base + down * 2 + core
    own_rb = f % 4
    sib_rb = sib % 4
    own_kk = z // 4
    matched = (kz % 2) == core

    def remote(src, dst, ssem, rsem, target):
        return pltpu.make_async_remote_copy(
            src_ref=src, dst_ref=dst, send_sem=ssem, recv_sem=rsem,
            device_id={"fsdp": target}, device_id_type=MESH,
        )

    loads = [
        pltpu.make_async_copy(x_ref.at[0], tok_x.at[2 * xh + core], load_sem.at[0]),
        pltpu.make_async_copy(d_ref.at[0], tok_d.at[2 * xh + core], load_sem.at[1]),
        pltpu.make_async_copy(mg_ref.at[0, 0], mom.at[0], load_sem.at[2]),
        pltpu.make_async_copy(mu_ref.at[0, 0], mom.at[1], load_sem.at[3]),
        pltpu.make_async_copy(md_ref.at[0, 0], mom.at[2], load_sem.at[4]),
        pltpu.make_async_copy(band_ref, band, load_sem.at[5]),
        pltpu.make_async_copy(table_ref, table, load_sem.at[6]),
    ]
    w_loads = [
        pltpu.make_async_copy(w.at[0], wts.at[own_kk, own_rb, m], load_sem.at[7 + m])
        for m, w in enumerate((wg_ref, wu_ref, wd_ref))
    ]

    @pl.when(matched)
    def _():
        for c in w_loads:
            c.start()
    for c in loads:
        c.start()

    barrier = pltpu.get_barrier_semaphore()
    others = [sib, partner] + [base + zz * 2 + c for zz in (up, down) for c in (0, 1)]
    for t in others:
        pl.semaphore_signal(barrier, inc=1, device_id={"fsdp": t}, device_id_type=MESH)
    for i in range(1, 8):
        pl.semaphore_signal(barrier, inc=1, device_id={"rep": (r + i) % 8}, device_id_type=MESH)
    pl.semaphore_wait(barrier, len(others) + 7)

    w_sib = [
        remote(w.at[0], wts.at[own_kk, own_rb, m], sib_sem.at[0, m], sib_sem.at[1, m], sib)
        for m, w in enumerate((wg_ref, wu_ref, wd_ref))
    ]

    @pl.when(jnp.logical_not(matched))
    def _():
        for c in w_sib:
            c.start()

    mine = 2 * xh + core
    theirs = 2 * (1 - xh) + core
    tok_copies = []
    for i, (src, dst) in enumerate(((x_ref, tok_x), (d_ref, tok_d))):
        tok_copies.append(remote(src.at[0], dst.at[mine], tok_send.at[0, i], tok_recv.at[0, i], partner))
    for i, (src, dst) in enumerate(((x_ref, tok_x), (d_ref, tok_d))):
        tok_copies.append(remote(src.at[0], dst.at[mine], tok_send.at[1, i], tok_recv.at[1, i], sib))
    for c in tok_copies:
        c.start()
    forwards = [
        remote(dst.at[theirs], dst.at[theirs], tok_send.at[2, i], tok_recv.at[2, i], sib)
        for i, dst in enumerate((tok_x, tok_d))
    ]

    @pl.when(matched)
    def _():
        for m in range(3):
            w_loads[m].wait()
            w_sib[m].wait_recv()

    @pl.when(jnp.logical_not(matched))
    def _():
        for m in range(3):
            w_sib[m].wait_send()

    def ag_chunk(way, s):
        src = (z + NZ - s) % NZ if way == 0 else (z + s) % NZ
        return (src // 2) % 2 == core, src // 4, (src % 2) * 2

    def ag_copy(way, s, kk, rb0, j):
        rb = rb0 + j // 3
        piece = wts.at[kk, rb, j % 3]
        return remote(
            piece, piece, ag_send.at[way, s, j], ag_recv.at[way, s, j], up_same if way == 0 else down_same
        )

    def ag_step(s, carry):
        for way in (0, 1):
            last = 8 - way
            active, kk, rb0 = ag_chunk(way, s)

            @pl.when(jnp.logical_and(active, s <= last))
            def _():
                for j in range(6):
                    @pl.when(s > 0)
                    def _():
                        ag_copy(way, s - 1, kk, rb0, j).wait_recv()

                    @pl.when(s < last)
                    def _():
                        ag_copy(way, s, kk, rb0, j).start()
        return carry

    lax.fori_loop(0, 9, ag_step, 0)

    for c in tok_copies[:2]:
        c.wait_recv()
    for c in forwards:
        c.start()
    for c in loads:
        c.wait()

    spots = lax.broadcasted_iota(jnp.int32, (SIDE, KEEP), 0)
    for m in range(3):
        at = band[m]
        pick_r[m] = jnp.where(spots == lax.shift_right_logical(at, 7), 1.0, 0.0).astype(BF16)
        pick_c[m] = jnp.where(spots == lax.bitwise_and(at, 127), 1.0, 0.0).astype(BF16)
    vals[...] = jnp.zeros((8, KEEP), F32)
    recv[:, 0] = jnp.zeros((2, 3, 2, QROWS, SIDE), jnp.int16)

    for c in tok_copies[2:]:
        c.wait_recv()
    for c in forwards:
        c.wait_recv()

    def column(kk):
        xs = tok_x[...].reshape(4 * SIDE, 4 * SIDE)
        ds = tok_d[...].reshape(4 * SIDE, 4 * SIDE)
        w_gu = jnp.concatenate(
            [wts[kk, :, 0].reshape(4 * SIDE, SIDE), wts[kk, :, 1].reshape(4 * SIDE, SIDE)], axis=1
        )
        w_d = jnp.concatenate([wts[kk, i, 2] for i in range(4)], axis=1)
        gu = mm(xs, w_gu, NN)
        dh = mm(ds, w_d, NT)
        gate = gu[:, :SIDE]
        upp = gu[:, SIDE:]
        sg = jax.nn.sigmoid(gate)
        act = gate * sg
        hidden = (act * upp).astype(BF16)
        d_gate = (dh * upp * sg * (1.0 + gate * (1.0 - sg))).astype(BF16)
        d_up = (dh * act).astype(BF16)
        g_in = mm(xs, jnp.concatenate([d_gate, d_up], axis=1), TN)
        g_out = mm(hidden, ds, TN)
        for i in range(4):
            part[kk, i, 0] = g_in[i * SIDE:(i + 1) * SIDE, :SIDE]
            part[kk, i, 1] = g_in[i * SIDE:(i + 1) * SIDE, SIDE:]
            part[kk, i, 2] = g_out[:, i * SIDE:(i + 1) * SIDE]

    def rs_chunk(way, s):
        dest = (z + 8 - s) % NZ if way == 0 else (z + 9 + s) % NZ
        return (dest // 2) % 2 == core, dest // 4, (dest % 2) * 2

    def rs_copy(way, s, m):
        return remote(
            send.at[way, s, m], recv.at[way, s + 1, m], rs_send.at[way, s, m, 0], rs_recv.at[way, s + 1, m],
            up_same if way == 0 else down_same,
        )

    def fin_copy(way, s, m, c):
        to = base + (up if way == 0 else down) * 2 + c
        return remote(
            send.at[way, s, m, c], fin.at[way, m], rs_send.at[way, s, m, c], fin_recv.at[way, m], to
        )

    own_copy = remote(part.at[own_kk, sib_rb], own, own_sem.at[0], own_sem.at[1], sib)

    def rs_step(t, carry):
        s = t - 1

        @pl.when(s >= 0)
        def _():
            for way in (0, 1):
                steps = 8 - way
                active, kk, rb0 = rs_chunk(way, s)

                @pl.when(jnp.logical_and(active, s < steps))
                def _():
                    for m in range(3):
                        @pl.when(s > 0)
                        def _():
                            rs_copy(way, s - 1, m).wait_recv()
                        for c in range(2):
                            total = part[kk, rb0 + c, m] + restore(recv.at[way, s, m, c])
                            quantize(total, send.at[way, s, m, c])

                        @pl.when(s < steps - 1)
                        def _():
                            rs_copy(way, s, m).start()

                        @pl.when(s == steps - 1)
                        def _():
                            for c in range(2):
                                fin_copy(way, s, m, c).start()

        @pl.when(t < 4)
        def _():
            off_m = jnp.where(t == 0, 4, jnp.where(t == 1, 2, jnp.where(t == 2, 6, 0)))
            off_u = jnp.where(t == 0, 5, jnp.where(t == 1, 3, jnp.where(t == 2, 1, 7)))
            k = (kz + jnp.where(matched, off_m, off_u)) % 8
            column(k // 2)

        @pl.when(jnp.logical_and(t == 3, matched))
        def _():
            own_copy.start()
            own[...] = part[own_kk, own_rb]
        return carry

    lax.fori_loop(0, 9, rs_step, 0)

    @pl.when(jnp.logical_not(matched))
    def _():
        own_copy.wait_recv()

    c_m = (table[0], table[1])
    ct_m = (table[2], table[3])
    moments = []
    coeffs = []
    for m in range(3):
        for way in (0, 1):
            fin_copy(way, 7 - way, m, core).wait_recv()
        total = own[m] + restore(fin.at[0, m]) + restore(fin.at[1, m])
        moment = 0.999 * mom[m] + total
        moments.append(moment)
        inner = mm3(c_m, split(moment), NN)
        coeff_t = mm3(c_m, split(inner), NT)
        coeffs.append(coeff_t)
        hi, lo = split(coeff_t)
        rows = mm(hi, pick_r[m], NN) + mm(lo, pick_r[m], NN)
        vals[m:m + 1, :] = jnp.sum(rows * pick_c[m].astype(F32), axis=0, keepdims=True)
    rep_copies = [
        pltpu.make_async_remote_copy(
            src_ref=vals, dst_ref=vals_all.at[r], send_sem=rep_send.at[i], recv_sem=rep_recv.at[r],
            device_id={"rep": (r + i) % 8}, device_id_type=MESH,
        )
        for i in range(1, 8)
    ]
    for c in rep_copies:
        c.start()
    vals_all[r] = vals[...]

    res = (rg_out, ru_out, rd_out)
    for m in range(3):
        mask = mm(pick_c[m], pick_r[m], NT)
        placed = jnp.where(mask > 0.5, coeffs[m], 0.0)
        half = mm3(ct_m, split(placed), NT)
        res[m][0, 0] = moments[m] - mm3(split(half), c_m, NN)

    for i in range(1, 8):
        q = (r + i) % 8
        pltpu.make_async_remote_copy(
            src_ref=vals, dst_ref=vals_all.at[q], send_sem=rep_send.at[i], recv_sem=rep_recv.at[q],
            device_id={"rep": q}, device_id_type=MESH,
        ).wait_recv()
    summed = vals_all[0]
    for i in range(1, 8):
        summed = summed + vals_all[i]
    for m, out in enumerate((ug_out, uu_out, ud_out)):
        hi, lo = split(summed[m:m + 1, :])
        cols = pick_c[m].astype(F32)
        placed = mm((cols * hi.astype(F32)).astype(BF16), pick_r[m], NT) + mm(
            (cols * lo.astype(F32)).astype(BF16), pick_r[m], NT
        )
        half = mm3(ct_m, split(placed), NT)
        out[0] = mm3(split(half), c_m, NN)

    for c in tok_copies + forwards + rep_copies:
        c.wait_send()

    @pl.when(matched)
    def _():
        own_copy.wait_send()

    def drain(s, carry):
        for way in (0, 1):
            steps = 8 - way
            active, kk, rb0 = ag_chunk(way, s)

            @pl.when(jnp.logical_and(active, s < steps))
            def _():
                for j in range(6):
                    ag_copy(way, s, kk, rb0, j).wait_send()
            sending, _, _ = rs_chunk(way, s)

            @pl.when(jnp.logical_and(sending, s < steps - 1))
            def _():
                for m in range(3):
                    rs_copy(way, s, m).wait_send()

            @pl.when(jnp.logical_and(sending, s == steps - 1))
            def _():
                for m in range(3):
                    for c in range(2):
                        fin_copy(way, s, m, c).wait_send()
        return carry

    lax.fori_loop(0, 8, drain, 0)


def per_device(x_in, d_out, gate_weight, up_weight, down_weight, mom_gate, mom_up, mom_down, band_index):
    dma = pltpu.SemaphoreType.DMA
    block = (SIDE, SIDE)
    scratch = [
        pltpu.VMEM((4, SIDE, 4 * SIDE), BF16),
        pltpu.VMEM((4, SIDE, 4 * SIDE), BF16),
        pltpu.VMEM((4, 4, 3) + block, BF16),
        pltpu.VMEM((4, 4, 3) + block, F32),
        pltpu.VMEM((2, 8, 3, 2, QROWS, SIDE), jnp.int16),
        pltpu.VMEM((2, 8, 3, 2, QROWS, SIDE), jnp.int16),
        pltpu.VMEM((2, 3, QROWS, SIDE), jnp.int16),
        pltpu.VMEM((3,) + block, F32),
        pltpu.VMEM((3,) + block, F32),
        pltpu.VMEM((3, 1, KEEP), jnp.int32),
        pltpu.VMEM((4,) + block, BF16),
        pltpu.VMEM((3, SIDE, KEEP), BF16),
        pltpu.VMEM((3, SIDE, KEEP), BF16),
        pltpu.VMEM((8, KEEP), F32),
        pltpu.VMEM((8, 8, KEEP), F32),
        dma((10,)),
        dma((3, 2)),
        dma((3, 2)),
        dma((2, 3)),
        dma((2, 8, 6)),
        dma((2, 8, 6)),
        dma((2, 8, 3, 2)),
        dma((2, 8, 3)),
        dma((2, 3)),
        dma((2,)),
        dma((8,)),
        dma((8,)),
    ]
    outs = [jax.ShapeDtypeStruct((1, 1) + block, F32)] * 3 + [jax.ShapeDtypeStruct((1,) + block, F32)] * 3
    return pl.pallas_call(
        kernel,
        out_shape=outs,
        in_specs=[pl.BlockSpec(memory_space=pl.ANY)] * 10,
        out_specs=[pl.BlockSpec(memory_space=pltpu.VMEM)] * 6,
        scratch_shapes=scratch,
        compiler_params=pltpu.CompilerParams(
            collective_id=0, has_side_effects=True, vmem_limit_bytes=48 * 1024 * 1024
        ),
        cost_estimate=pl.CostEstimate(flops=1700000000, bytes_accessed=2000000, transcendentals=300000),
    )(
        x_in, d_out, gate_weight, up_weight, down_weight, mom_gate, mom_up, mom_down, band_index,
        jnp.asarray(dct_parts()),
    )


def solution(mesh):
    tokens = P("rep", "fsdp", None)
    weights = P("fsdp", None, None)
    moments = P("rep", "fsdp", None, None)
    return jax.shard_map(
        per_device, mesh=mesh,
        in_specs=(tokens, tokens, weights, weights, weights, moments, moments, moments, P(None, "fsdp", None)),
        out_specs=(moments, moments, moments, weights, weights, weights),
        check_vma=False,
    )
```

```python
import jax
import jax.numpy as jnp
import numpy as np
from jax import lax
from jax.experimental import pallas as pl
from jax.experimental.pallas import tpu as pltpu
from jax.sharding import PartitionSpec as P

MESH = pl.DeviceIdType.MESH
F32 = jnp.float32
BF16 = jnp.bfloat16
SIDE = 128
WIDE = 512
KEEP = 512
NZ = 16
HALF = SIDE // 2
PIECES = 12


def dct_parts():
    k = np.arange(SIDE, dtype=np.float64)[:, None]
    n = np.arange(SIDE, dtype=np.float64)[None, :]
    s = np.where(k == 0, np.sqrt(1.0 / SIDE), np.sqrt(2.0 / SIDE))
    c = (s * np.cos(np.pi * (2.0 * n + 1.0) * k / (2.0 * SIDE))).astype(np.float32)
    out = []
    for t in (c, c.T):
        hi = t.astype(jnp.bfloat16)
        lo = (t - hi.astype(np.float32)).astype(jnp.bfloat16)
        out += [hi, lo]
    return np.stack(out)


def mm(a, b, dims):
    return lax.dot_general(a, b, (dims, ((), ())), preferred_element_type=F32)


NN = ((1,), (0,))
NT = ((1,), (1,))
TN = ((0,), (0,))


def split(a):
    hi = a.astype(BF16)
    return hi, (a - hi.astype(F32)).astype(BF16)


def mm3(a, b, dims):
    return mm(a[0], b[0], dims) + (mm(a[0], b[1], dims) + mm(a[1], b[0], dims))


def kernel(
    x_ref, d_ref, wg_ref, wu_ref, wd_ref, mg_ref, mu_ref, md_ref, band_ref, table_ref,
    out,
    tok, mine_w, wts, part, recv, send, fin, mom, band, table, pick_r, pick_c, mask, vals, vals_all,
    load_sem, tok_send, tok_recv, w1_send, w1_recv, w2_send, w2_recv, rs_send, rs_recv, fin_recv,
    rep_send, rep_recv,
):
    f = lax.axis_index("fsdp")
    r = lax.axis_index("rep")
    core = f % 2
    z = (f // 2) % NZ
    xh = f // (2 * NZ)
    base = xh * (2 * NZ)
    sib = f + 1 - 2 * core
    partner = f + (1 - 2 * xh) * (2 * NZ)
    m_own = z // 2
    p_own = z % 2

    def chip(zz, c):
        return base + ((zz + NZ) % NZ) * 2 + c

    def remote(src, dst, ssem, rsem, target):
        return pltpu.make_async_remote_copy(
            src_ref=src, dst_ref=dst, send_sem=ssem, recv_sem=rsem,
            device_id={"fsdp": target}, device_id_type=MESH,
        )

    def to_rep(src, dst, ssem, rsem, target):
        return pltpu.make_async_remote_copy(
            src_ref=src, dst_ref=dst, send_sem=ssem, recv_sem=rsem,
            device_id={"rep": target}, device_id_type=MESH,
        )

    recv[...] = jnp.zeros(recv.shape, BF16)
    barrier = pltpu.get_barrier_semaphore()

    def greet(i, carry):
        pl.semaphore_signal(
            barrier, inc=1, device_id={"fsdp": base + (f - base + i) % (2 * NZ)}, device_id_type=MESH
        )
        return carry

    lax.fori_loop(1, 2 * NZ, greet, 0)
    pl.semaphore_signal(barrier, inc=1, device_id={"fsdp": partner}, device_id_type=MESH)
    for i in range(1, 8):
        pl.semaphore_signal(barrier, inc=1, device_id={"rep": (r + i) % 8}, device_id_type=MESH)

    slot = pl.multiple_of((2 * xh + core) * 2 * SIDE, 2 * SIDE)
    other = pl.multiple_of((2 * (1 - xh) + core) * 2 * SIDE, 2 * SIDE)
    loads = [
        pltpu.make_async_copy(band_ref, band, load_sem.at[0]),
        pltpu.make_async_copy(wg_ref.at[0], mine_w.at[0], load_sem.at[1]),
        pltpu.make_async_copy(wu_ref.at[0], mine_w.at[1], load_sem.at[2]),
        pltpu.make_async_copy(wd_ref.at[0], mine_w.at[2], load_sem.at[3]),
        pltpu.make_async_copy(x_ref.at[0], tok.at[0, pl.ds(slot, SIDE)], load_sem.at[4]),
        pltpu.make_async_copy(d_ref.at[0], tok.at[1, pl.ds(slot, SIDE)], load_sem.at[5]),
        pltpu.make_async_copy(mg_ref.at[0, 0], mom.at[0], load_sem.at[6]),
        pltpu.make_async_copy(mu_ref.at[0, 0], mom.at[1], load_sem.at[7]),
        pltpu.make_async_copy(md_ref.at[0, 0], mom.at[2], load_sem.at[8]),
        pltpu.make_async_copy(table_ref, table, load_sem.at[9]),
    ]
    for c in loads:
        c.start()

    vals[...] = jnp.zeros(vals.shape, F32)
    loads[0].wait()
    spots = lax.broadcasted_iota(jnp.int32, (SIDE, KEEP), 0)
    for m in range(3):
        at = band[m]
        pick_r[m] = jnp.where(spots == lax.shift_right_logical(at, 7), 1.0, 0.0).astype(BF16)
        pick_c[m] = jnp.where(spots == lax.bitwise_and(at, 127), 1.0, 0.0).astype(BF16)
    for m in range(3):
        mask[m] = mm(pick_c[m], pick_r[m], NT)
    for c in loads[1:]:
        c.wait()

    k_own = z // 2
    h_own = k_own % 2
    kk_own = (k_own % 4) // 2
    rb_own = f % 4
    eighth = pl.ds(pl.multiple_of(r * 16, 16), 16)
    skew = jnp.where(p_own == k_own // 4, 0, 1)

    def w1_copy(i, target):
        return remote(
            mine_w.at[:, eighth], wts.at[kk_own, rb_own, :, eighth], w1_send.at[i], w1_recv.at[kk_own, rb_own], target
        )

    hops = (8, -6, 6, -4, 4, -2, 2, 0)
    w1_to = [chip(z + hop + skew, h_own) for hop in hops]
    w1_self = w1_to[-1] == f

    @pl.when(w1_self)
    def _():
        wts[kk_own, rb_own, :, eighth, :] = mine_w[:, eighth, :]

    pl.semaphore_wait(barrier, 2 * NZ + 7)

    for i, target in enumerate(w1_to[:-1]):
        w1_copy(i, target).start()

    @pl.when(jnp.logical_not(w1_self))
    def _():
        w1_copy(7, w1_to[-1]).start()

    def rows(start, size):
        return tok.at[:, pl.ds(start, size)]

    def tok_copy(i, src, dst, size, target):
        return remote(rows(src, size), rows(dst, size), tok_send.at[i], tok_recv.at[i], target)

    up = chip(z + 1, core)
    down = chip(z - 1, core)
    to_partner = tok_copy(0, slot, slot, SIDE, partner)
    to_up = tok_copy(1, slot, slot + SIDE, HALF, up)
    to_down = tok_copy(2, slot + HALF, slot + SIDE + HALF, HALF, down)
    to_sib = tok_copy(3, slot, slot, SIDE, sib)
    for c in (to_partner, to_up, to_down, to_sib):
        c.start()
    from_partner = tok_copy(0, slot, other, SIDE, partner)
    on_up = tok_copy(4, other, other + SIDE, HALF, up)
    on_down = tok_copy(5, other + HALF, other + SIDE + HALF, HALF, down)
    on_sib = tok_copy(6, other, other, SIDE, sib)
    near_sib = tok_copy(7, slot + SIDE, slot + SIDE, SIDE, sib)
    far_sib = tok_copy(8, other + SIDE, other + SIDE, SIDE, sib)

    def column_of(kk):
        k = 4 * p_own + core + 2 * kk
        ahead = (k - m_own + 8) % 8
        return k, ahead, jnp.where(ahead > 4, ahead - 4, 4 - ahead)

    stage_0 = column_of(0)[2]
    stage_1 = column_of(1)[2]
    first = jnp.where(stage_0 <= stage_1, 0, 1)
    stage_first = jnp.minimum(stage_0, stage_1)
    together = stage_0 == stage_1

    def w2_copy(kk, i):
        piece = wts.at[kk, :, :, eighth]
        return to_rep(piece, piece, w2_send.at[kk, i], w2_recv.at[kk, r], (r + i) % 8)

    def w1_arrived(kk):
        k = column_of(kk)[0]
        for rb in range(4):
            @pl.when(base + 4 * k + rb != f)
            def _():
                remote(
                    mine_w.at[:, eighth], wts.at[kk, rb, :, eighth], w1_send.at[0], w1_recv.at[kk, rb], sib
                ).wait_recv()
        for i in range(1, 8):
            w2_copy(kk, i).start()

    w1_arrived(1 - first)
    from_partner.wait_recv()
    for c in (on_up, on_down, on_sib):
        c.start()
    w1_arrived(first)
    to_up.wait_recv()
    to_down.wait_recv()
    near_sib.start()
    on_up.wait_recv()
    on_down.wait_recv()
    far_sib.start()
    for c in (to_sib, on_sib, near_sib, far_sib):
        c.wait_recv()

    def column(kk):
        xs = tok[0]
        ds = tok[1]
        w_gu = jnp.concatenate(
            [wts[kk, :, 0].reshape(WIDE, SIDE), wts[kk, :, 1].reshape(WIDE, SIDE)], axis=1
        )
        w_d = jnp.concatenate([wts[kk, i, 2] for i in range(4)], axis=1)
        gu = mm(xs, w_gu, NN)
        dh = mm(ds, w_d, NT)
        gate = gu[:, :SIDE]
        upp = gu[:, SIDE:]
        sg = jax.nn.sigmoid(gate)
        act = gate * sg
        hidden = (act * upp).astype(BF16)
        d_gate = (dh * upp * sg * (1.0 + gate * (1.0 - sg))).astype(BF16)
        d_up = (dh * act).astype(BF16)
        g_in = mm(xs, jnp.concatenate([d_gate, d_up], axis=1), TN)
        g_out = mm(hidden, ds, TN)
        for i in range(4):
            part[kk, i, 0] = g_in[i * SIDE:(i + 1) * SIDE, :SIDE]
            part[kk, i, 1] = g_in[i * SIDE:(i + 1) * SIDE, SIDE:]
            part[kk, i, 2] = g_out[:, i * SIDE:(i + 1) * SIDE]

    def on_copy(kk, rb, m, target):
        return remote(send.at[kk, rb, m], recv.at[kk, rb, m], rs_send.at[kk, rb, m], rs_recv.at[kk, rb, m], target)

    def fin_copy(kk, rb, m, way, target):
        return remote(send.at[kk, rb, m], fin.at[way, m], rs_send.at[kk, rb, m], fin_recv.at[way, m], target)

    def pass_on(kk, j):
        m = j // 4
        rb = j % 4
        k, ahead, stage = column_of(kk)
        low = rb < 2
        heard = (
            (ahead == 1) | (ahead == 2) | (ahead == 6) | (ahead == 7)
            | ((ahead == 3) & low) | ((ahead == 5) & jnp.logical_not(low))
        )
        upward = (ahead < 4) | ((ahead == 4) & low)
        last = (ahead == 0) | (ahead == 1) | (ahead == 7)
        owner = base + 4 * k + rb

        @pl.when(heard)
        def _():
            on_copy(kk, rb, m, sib).wait_recv()
        value = (part[kk, rb, m] + recv[kk, rb, m].astype(F32)).astype(BF16)
        send[kk, rb, m] = value

        @pl.when(jnp.logical_not(last))
        def _():
            on_copy(kk, rb, m, jnp.where(upward, chip(z + 2, core), chip(z - 2, core))).start()

        @pl.when(last & (owner != f))
        def _():
            way = jnp.where(ahead == 0, 2, jnp.where(ahead == 1, 0, 1))
            fin_copy(kk, rb, m, way, owner).start()

        @pl.when(last & (owner == f))
        def _():
            fin[2, m] = value

    def pass_all(j, carry):
        pass_on(first, j)
        return carry

    def work(i, carry):
        kk = jnp.where(i == 0, first, 1 - first)
        for q in range(1, 8):
            w2_in = wts.at[kk, :, :, eighth]
            to_rep(w2_in, w2_in, w2_send.at[kk, q], w2_recv.at[kk, (r + q) % 8], r).wait_recv()
        column(kk)

        @pl.when((i == 0) & (stage_first == 0))
        def _():
            lax.fori_loop(0, PIECES, pass_all, 0)
        return carry

    lax.fori_loop(0, 2, work, 0)

    def pass_rest(t, carry):
        second = jnp.where(together, t % 2, t // PIECES)
        j = jnp.where(together, t // 2, t % PIECES)
        pass_on(jnp.where(second == 0, first, 1 - first), j)
        return carry

    lax.fori_loop(jnp.where(stage_first == 0, PIECES, 0), 2 * PIECES, pass_rest, 0)

    c_m = (table[0], table[1])
    ct_m = (table[2], table[3])
    is_middle = (m_own == k_own) & (p_own == k_own // 4) & (core == h_own)
    moments = []
    coeffs = []
    for m in range(3):
        for way in (0, 1):
            fin_copy(0, 0, m, way, sib).wait_recv()

        @pl.when(jnp.logical_not(is_middle))
        def _():
            fin_copy(0, 0, m, 2, sib).wait_recv()
        total = fin[0, m].astype(F32) + fin[1, m].astype(F32) + fin[2, m].astype(F32)
        moment = 0.999 * mom[m] + total
        moments.append(moment)
        inner = mm3(c_m, split(moment), NN)
        coeff_t = mm3(c_m, split(inner), NT)
        coeffs.append(coeff_t)
        hi, lo = split(coeff_t)
        picked = mm(hi, pick_r[m], NN) + mm(lo, pick_r[m], NN)
        vals[m:m + 1, :] = jnp.sum(picked * pick_c[m].astype(F32), axis=0, keepdims=True)
    rep_copies = [to_rep(vals, vals_all.at[r], rep_send.at[i], rep_recv.at[r], (r + i) % 8) for i in range(1, 8)]
    for c in rep_copies:
        c.start()
    vals_all[r] = vals[...]

    for m in range(3):
        placed = jnp.where(mask[m] > 0.5, coeffs[m], 0.0)
        half = mm3(ct_m, split(placed), NT)
        out[m] = moments[m] - mm3(split(half), c_m, NN)

    for i in range(1, 8):
        q = (r + i) % 8
        to_rep(vals, vals_all.at[q], rep_send.at[i], rep_recv.at[q], q).wait_recv()
    summed = vals_all[0]
    for i in range(1, 8):
        summed = summed + vals_all[i]
    for m in range(3):
        hi, lo = split(summed[m:m + 1, :])
        cols = pick_c[m].astype(F32)
        placed = mm((cols * hi.astype(F32)).astype(BF16), pick_r[m], NT) + mm(
            (cols * lo.astype(F32)).astype(BF16), pick_r[m], NT
        )
        half = mm3(ct_m, split(placed), NT)
        out[3 + m] = mm3(split(half), c_m, NN)

    for c in (to_partner, to_up, to_down, to_sib, on_up, on_down, on_sib, near_sib, far_sib):
        c.wait_send()
    for c in rep_copies:
        c.wait_send()
    for i, target in enumerate(w1_to[:-1]):
        w1_copy(i, target).wait_send()

    @pl.when(jnp.logical_not(w1_self))
    def _():
        w1_copy(7, w1_to[-1]).wait_send()

    def drain(kk, carry):
        k = column_of(kk)[0]
        for i in range(1, 8):
            w2_copy(kk, i).wait_send()
        for j in range(PIECES):
            @pl.when(base + 4 * k + j % 4 != f)
            def _():
                on_copy(kk, j % 4, j // 4, sib).wait_send()
        return carry

    lax.fori_loop(0, 2, drain, 0)


def write_out(all_ref, *refs):
    outs, sems = refs[:6], refs[6]
    copies = [
        pltpu.make_async_copy(all_ref.at[i], o.at[(0, 0) if i < 3 else (0,)], sems.at[i]) for i, o in enumerate(outs)
    ]
    for c in copies:
        c.start()
    for c in copies:
        c.wait()


def per_device(x_in, d_out, gate_weight, up_weight, down_weight, mom_gate, mom_up, mom_down, band_index):
    dma = pltpu.SemaphoreType.DMA
    block = (SIDE, SIDE)
    scratch = [
        pltpu.VMEM((2, 8 * SIDE, WIDE), BF16),
        pltpu.VMEM((3,) + block, BF16),
        pltpu.VMEM((2, 4, 3) + block, BF16),
        pltpu.VMEM((2, 4, 3) + block, F32),
        pltpu.VMEM((2, 4, 3) + block, BF16),
        pltpu.VMEM((2, 4, 3) + block, BF16),
        pltpu.VMEM((3, 3) + block, BF16),
        pltpu.VMEM((3,) + block, F32),
        pltpu.VMEM((3, 1, KEEP), jnp.int32),
        pltpu.VMEM((4,) + block, BF16),
        pltpu.VMEM((3, SIDE, KEEP), BF16),
        pltpu.VMEM((3, SIDE, KEEP), BF16),
        pltpu.VMEM((3,) + block, F32),
        pltpu.VMEM((8, KEEP), F32),
        pltpu.VMEM((8, 8, KEEP), F32),
        dma((10,)),
        dma((9,)),
        dma((9,)),
        dma((8,)),
        dma((2, 4)),
        dma((2, 8)),
        dma((2, 8)),
        dma((2, 4, 3)),
        dma((2, 4, 3)),
        dma((3, 3)),
        dma((8,)),
        dma((8,)),
    ]
    hbm = pl.BlockSpec(memory_space=pltpu.HBM)
    vmem = pl.BlockSpec(memory_space=pltpu.VMEM)
    results = pl.pallas_call(
        kernel,
        out_shape=jax.ShapeDtypeStruct((6,) + block, F32),
        in_specs=[hbm] * 10,
        out_specs=vmem,
        scratch_shapes=scratch,
        compiler_params=pltpu.CompilerParams(
            collective_id=0, has_side_effects=True, vmem_limit_bytes=62 * 1024 * 1024
        ),
        cost_estimate=pl.CostEstimate(flops=1700000000, bytes_accessed=2000000, transcendentals=300000),
    )(
        x_in, d_out, gate_weight, up_weight, down_weight, mom_gate, mom_up, mom_down, band_index,
        jnp.asarray(dct_parts()),
    )
    outs = [jax.ShapeDtypeStruct((1, 1) + block, F32)] * 3 + [jax.ShapeDtypeStruct((1,) + block, F32)] * 3
    return pl.pallas_call(
        write_out, out_shape=outs, in_specs=[vmem], out_specs=[hbm] * 6, scratch_shapes=[dma((6,))]
    )(results)


def solution(mesh):
    tokens = P("rep", "fsdp", None)
    weights = P("fsdp", None, None)
    moments = P("rep", "fsdp", None, None)
    return jax.shard_map(
        per_device, mesh=mesh,
        in_specs=(tokens, tokens, weights, weights, weights, moments, moments, moments, P(None, "fsdp", None)),
        out_specs=(moments, moments, moments, weights, weights, weights),
        check_vma=False,
    )
```

```python
import jax
import jax.numpy as jnp
import numpy as np
from jax import lax
from jax.experimental import pallas as pl
from jax.experimental.pallas import tpu as pltpu
from jax.sharding import PartitionSpec as P

MESH = pl.DeviceIdType.MESH
F32 = jnp.float32
BF16 = jnp.bfloat16
SIDE = 128
WIDE = 512
KEEP = 512
NZ = 16
HALF = SIDE // 2
PIECES = 12


def dct_parts():
    k = np.arange(SIDE, dtype=np.float64)[:, None]
    n = np.arange(SIDE, dtype=np.float64)[None, :]
    s = np.where(k == 0, np.sqrt(1.0 / SIDE), np.sqrt(2.0 / SIDE))
    c = (s * np.cos(np.pi * (2.0 * n + 1.0) * k / (2.0 * SIDE))).astype(np.float32)
    out = []
    for t in (c, c.T):
        hi = t.astype(jnp.bfloat16)
        lo = (t - hi.astype(np.float32)).astype(jnp.bfloat16)
        out += [hi, lo]
    return np.stack(out)


def mm(a, b, dims):
    return lax.dot_general(a, b, (dims, ((), ())), preferred_element_type=F32)


NN = ((1,), (0,))
NT = ((1,), (1,))
TN = ((0,), (0,))


def split(a):
    hi = a.astype(BF16)
    return hi, (a - hi.astype(F32)).astype(BF16)


def mm3(a, b, dims):
    return mm(a[0], b[0], dims) + (mm(a[0], b[1], dims) + mm(a[1], b[0], dims))


def kernel(
    x_ref, d_ref, wg_ref, wu_ref, wd_ref, mg_ref, mu_ref, md_ref, band_ref, table_ref,
    out,
    tok, mine_w, wts, part, recv, send, fin, mom, band, table, pick_r, pick_c, mask, vals, vals_all,
    load_sem, tok_send, tok_recv, w1_send, w1_recv, w2_send, w2_recv, rs_send, rs_recv, fin_recv,
    rep_send, rep_recv,
):
    f = lax.axis_index("fsdp")
    r = lax.axis_index("rep")
    core = f % 2
    z = (f // 2) % NZ
    xh = f // (2 * NZ)
    base = xh * (2 * NZ)
    sib = f + 1 - 2 * core
    partner = f + (1 - 2 * xh) * (2 * NZ)
    m_own = z // 2
    p_own = z % 2

    def chip(zz, c):
        return base + ((zz + NZ) % NZ) * 2 + c

    def remote(src, dst, ssem, rsem, target):
        return pltpu.make_async_remote_copy(
            src_ref=src, dst_ref=dst, send_sem=ssem, recv_sem=rsem,
            device_id={"fsdp": target}, device_id_type=MESH,
        )

    def to_rep(src, dst, ssem, rsem, target):
        return pltpu.make_async_remote_copy(
            src_ref=src, dst_ref=dst, send_sem=ssem, recv_sem=rsem,
            device_id={"rep": target}, device_id_type=MESH,
        )

    k_own = z // 2
    h_own = (k_own // 2) % 2
    kk_own = k_own // 4
    rb_own = f % 4
    skew = jnp.where(p_own == k_own % 2, 0, 1)
    w1_to = [chip(z + hop + skew, h_own) for hop in (8, -6, 6, -4, 4, -2, 2, 0)]
    w1_self = w1_to[-1] == f

    recv[...] = jnp.zeros(recv.shape, BF16)
    barrier = pltpu.get_barrier_semaphore()

    def greet(**to):
        pl.semaphore_signal(barrier, inc=1, device_id=to, device_id_type=MESH)

    sources = [base + 4 * (p_own + 2 * core + 4 * kk) + rb for kk in (0, 1) for rb in range(4)]
    for target in w1_to[:-1]:
        greet(fsdp=target)
    for source in sources + [w1_to[-1]]:
        @pl.when(source != f)
        def _():
            greet(fsdp=source)
    near = [chip(z + 2, core), chip(z - 2, core), chip(z + 1, core), chip(z - 1, core), partner, sib]
    for target in near:
        greet(fsdp=target)
    for i in range(1, 8):
        greet(rep=(r + i) % 8)

    slot = pl.multiple_of((2 * xh + core) * 2 * SIDE, 2 * SIDE)
    other = pl.multiple_of((2 * (1 - xh) + core) * 2 * SIDE, 2 * SIDE)
    loads = [
        pltpu.make_async_copy(band_ref, band, load_sem.at[0]),
        pltpu.make_async_copy(wg_ref.at[0], mine_w.at[0], load_sem.at[1]),
        pltpu.make_async_copy(wu_ref.at[0], mine_w.at[1], load_sem.at[2]),
        pltpu.make_async_copy(wd_ref.at[0], mine_w.at[2], load_sem.at[3]),
        pltpu.make_async_copy(x_ref.at[0], tok.at[0, pl.ds(slot, SIDE)], load_sem.at[4]),
        pltpu.make_async_copy(d_ref.at[0], tok.at[1, pl.ds(slot, SIDE)], load_sem.at[5]),
        pltpu.make_async_copy(mg_ref.at[0, 0], mom.at[0], load_sem.at[6]),
        pltpu.make_async_copy(mu_ref.at[0, 0], mom.at[1], load_sem.at[7]),
        pltpu.make_async_copy(md_ref.at[0, 0], mom.at[2], load_sem.at[8]),
        pltpu.make_async_copy(table_ref, table, load_sem.at[9]),
    ]
    for c in loads:
        c.start()

    vals[...] = jnp.zeros(vals.shape, F32)
    loads[0].wait()
    spots = lax.broadcasted_iota(jnp.int32, (SIDE, KEEP), 0)
    for m in range(3):
        at = band[m]
        pick_r[m] = jnp.where(spots == lax.shift_right_logical(at, 7), 1.0, 0.0).astype(BF16)
        pick_c[m] = jnp.where(spots == lax.bitwise_and(at, 127), 1.0, 0.0).astype(BF16)
    for m in range(3):
        mask[m] = mm(pick_c[m], pick_r[m], NT)
    for c in loads[1:]:
        c.wait()

    eighth = pl.ds(pl.multiple_of(r * 16, 16), 16)

    def w1_copy(i, target):
        return remote(
            mine_w.at[:, eighth], wts.at[kk_own, r, rb_own], w1_send.at[i], w1_recv.at[kk_own, rb_own], target
        )

    @pl.when(w1_self)
    def _():
        wts[kk_own, r, rb_own] = mine_w[:, eighth, :]

    pl.semaphore_wait(barrier, jnp.where(w1_self, 27, 29))

    for i, target in enumerate(w1_to[:-1]):
        w1_copy(i, target).start()

    @pl.when(jnp.logical_not(w1_self))
    def _():
        w1_copy(7, w1_to[-1]).start()

    def rows(start, size):
        return tok.at[:, pl.ds(start, size)]

    def tok_copy(i, src, dst, size, target):
        return remote(rows(src, size), rows(dst, size), tok_send.at[i], tok_recv.at[i], target)

    up = chip(z + 1, core)
    down = chip(z - 1, core)
    quarter = HALF // 2
    parts = [(0, up, SIDE), (HALF, down, SIDE), (quarter, up, SIDE), (HALF + quarter, down, SIDE)]
    to_partner = [tok_copy(i, slot + at, slot + at, quarter, partner) for i, (at, _, _) in enumerate(parts)]
    from_partner = [tok_copy(i, slot + at, other + at, quarter, partner) for i, (at, _, _) in enumerate(parts)]
    pass_near = [tok_copy(4 + i, other + at, other + at + off, quarter, to) for i, (at, to, off) in enumerate(parts)]
    pass_far = [tok_copy(8 + i, other + at + off, other + at + off, quarter, sib) for i, (at, _, off) in enumerate(parts)]
    to_up = tok_copy(12, slot, slot + SIDE, HALF, up)
    to_down = tok_copy(13, slot + HALF, slot + SIDE + HALF, HALF, down)
    to_sib = tok_copy(14, slot, slot, SIDE, sib)
    on_sib = tok_copy(15, other, other, SIDE, sib)
    near_sib = tok_copy(16, slot + SIDE, slot + SIDE, SIDE, sib)
    for c in to_partner + [to_up, to_down, to_sib]:
        c.start()

    def column_of(kk):
        k = p_own + 2 * core + 4 * kk
        ahead = (k - m_own + 8) % 8
        return k, ahead, jnp.where(ahead > 4, ahead - 4, 4 - ahead)

    stage_0 = column_of(0)[2]
    stage_1 = column_of(1)[2]
    first = jnp.where(stage_0 <= stage_1, 0, 1)

    def w2_copy(kk, i):
        piece = wts.at[kk, r]
        return to_rep(piece, piece, w2_send.at[kk, i], w2_recv.at[kk, r], (r + i) % 8)

    def w1_arrived(kk):
        k = column_of(kk)[0]
        for rb in range(4):
            @pl.when(base + 4 * k + rb != f)
            def _():
                remote(
                    mine_w.at[:, eighth], wts.at[kk, r, rb], w1_send.at[0], w1_recv.at[kk, rb], sib
                ).wait_recv()
        for i in range(1, 8):
            w2_copy(kk, i).start()

    def tokens_in(i):
        from_partner[i].wait_recv()
        pass_near[i].start()

    for i in range(3):
        tokens_in(i)
    w1_arrived(first)
    tokens_in(3)
    on_sib.start()
    to_up.wait_recv()
    to_down.wait_recv()
    near_sib.start()
    w1_arrived(1 - first)
    for c, d in zip(pass_near, pass_far):
        c.wait_recv()
        d.start()
    for c in [to_sib, on_sib, near_sib] + pass_far:
        c.wait_recv()

    def column(kk):
        xs = tok[0]
        ds = tok[1]
        w_g, w_u, w_d = ([wts[kk, :, i, m].reshape(SIDE, SIDE) for i in range(4)] for m in range(3))
        w_gu = jnp.concatenate([jnp.concatenate(w_g, axis=0), jnp.concatenate(w_u, axis=0)], axis=1)
        w_d = jnp.concatenate(w_d, axis=1)
        gu = mm(xs, w_gu, NN)
        dh = mm(ds, w_d, NT)
        gate = gu[:, :SIDE]
        upp = gu[:, SIDE:]
        sg = jax.nn.sigmoid(gate)
        act = gate * sg
        hidden = (act * upp).astype(BF16)
        d_gate = (dh * upp * sg * (1.0 + gate * (1.0 - sg))).astype(BF16)
        d_up = (dh * act).astype(BF16)
        g_in = mm(xs, jnp.concatenate([d_gate, d_up], axis=1), TN)
        g_out = mm(hidden, ds, TN)
        for i in range(4):
            part[kk, i, 0] = g_in[i * SIDE:(i + 1) * SIDE, :SIDE]
            part[kk, i, 1] = g_in[i * SIDE:(i + 1) * SIDE, SIDE:]
            part[kk, i, 2] = g_out[:, i * SIDE:(i + 1) * SIDE]

    def on_copy(kk, rb, m, target):
        return remote(send.at[kk, rb, m], recv.at[kk, rb, m], rs_send.at[kk, rb, m], rs_recv.at[kk, rb, m], target)

    def fin_copy(kk, rb, m, way, target):
        return remote(send.at[kk, rb, m], fin.at[way, m], rs_send.at[kk, rb, m], fin_recv.at[way, m], target)

    def turn_of(ahead, half):
        up_turn = 4 - half - ahead
        down_turn = ahead - 5 + half
        return jnp.where(ahead == 0, 4, jnp.where(ahead < 4, up_turn, jnp.where(ahead == 4, 0, down_turn)))

    def pass_on(kk, half, j):
        m = j // 2
        rb = 2 * half + j % 2
        k, ahead, stage = column_of(kk)
        heard = (turn_of(ahead, half) > 0) & (ahead != 0)
        upward = (ahead < 4) | ((ahead == 4) & (half == 0))
        last = (ahead == 0) | (ahead == 1) | (ahead == 7)
        owner = base + 4 * k + rb

        @pl.when(heard)
        def _():
            on_copy(kk, rb, m, sib).wait_recv()
        value = (part[kk, rb, m] + recv[kk, rb, m].astype(F32)).astype(BF16)
        send[kk, rb, m] = value

        @pl.when(jnp.logical_not(last))
        def _():
            on_copy(kk, rb, m, jnp.where(upward, chip(z + 2, core), chip(z - 2, core))).start()

        @pl.when(last & (owner != f))
        def _():
            way = jnp.where(ahead == 0, 2, jnp.where(ahead == 1, 0, 1))
            fin_copy(kk, rb, m, way, owner).start()

        @pl.when(last & (owner == f))
        def _():
            fin[2, m] = value

    def pass_turn(kks, turn):
        halves = [(kk, half) for kk in kks for half in (0, 1)]
        due = [turn_of(column_of(kk)[1], half) == turn for kk, half in halves]

        def step(j, carry):
            for (kk, half), now in zip(halves, due):
                @pl.when(now)
                def _():
                    pass_on(kk, half, j)
            return carry

        lax.fori_loop(0, PIECES // 2, step, 0)

    def work(i, carry):
        kk = jnp.where(i == 0, first, 1 - first)
        for q in range(1, 8):
            w2_in = wts.at[kk, (r + q) % 8]
            to_rep(w2_in, w2_in, w2_send.at[kk, q], w2_recv.at[kk, (r + q) % 8], r).wait_recv()
        column(kk)

        pass_turn((kk,), 0)
        return carry

    lax.fori_loop(0, 2, work, 0)

    def pass_rest(turn, carry):
        pass_turn((first, 1 - first), turn)
        return carry

    lax.fori_loop(1, 5, pass_rest, 0)

    c_m = (table[0], table[1])
    ct_m = (table[2], table[3])
    is_middle = (m_own == k_own) & (p_own == k_own % 2) & (core == h_own)
    moments = []
    coeffs = []
    for m in range(3):
        for way in (0, 1):
            fin_copy(0, 0, m, way, sib).wait_recv()

        @pl.when(jnp.logical_not(is_middle))
        def _():
            fin_copy(0, 0, m, 2, sib).wait_recv()
        total = fin[0, m].astype(F32) + fin[1, m].astype(F32) + fin[2, m].astype(F32)
        moment = 0.999 * mom[m] + total
        moments.append(moment)
        inner = mm3(c_m, split(moment), NN)
        coeff_t = mm3(c_m, split(inner), NT)
        coeffs.append(coeff_t)
        hi, lo = split(coeff_t)
        picked = mm(hi, pick_r[m], NN) + mm(lo, pick_r[m], NN)
        band_row = jnp.sum(picked * pick_c[m].astype(F32), axis=0, keepdims=True)
        for q in range(4):
            vals[4 * m + q:4 * m + q + 1, :] = band_row[:, q * SIDE:(q + 1) * SIDE]
    rep_copies = [to_rep(vals, vals_all.at[r], rep_send.at[i], rep_recv.at[r], (r + i) % 8) for i in range(1, 8)]
    for c in rep_copies:
        c.start()
    vals_all[r] = vals[...]

    for m in range(3):
        placed = jnp.where(mask[m] > 0.5, coeffs[m], 0.0)
        half = mm3(ct_m, split(placed), NT)
        out[m] = moments[m] - mm3(split(half), c_m, NN)

    for i in range(1, 8):
        q = (r + i) % 8
        to_rep(vals, vals_all.at[q], rep_send.at[i], rep_recv.at[q], q).wait_recv()
    summed = vals_all[0]
    for i in range(1, 8):
        summed = summed + vals_all[i]
    for m in range(3):
        hi, lo = split(jnp.concatenate([summed[4 * m + q:4 * m + q + 1, :] for q in range(4)], axis=1))
        cols = pick_c[m].astype(F32)
        placed = mm((cols * hi.astype(F32)).astype(BF16), pick_r[m], NT) + mm(
            (cols * lo.astype(F32)).astype(BF16), pick_r[m], NT
        )
        half = mm3(ct_m, split(placed), NT)
        out[3 + m] = mm3(split(half), c_m, NN)

    for c in to_partner + pass_near + pass_far + [to_up, to_down, to_sib, on_sib, near_sib]:
        c.wait_send()
    for c in rep_copies:
        c.wait_send()
    for i, target in enumerate(w1_to[:-1]):
        w1_copy(i, target).wait_send()

    @pl.when(jnp.logical_not(w1_self))
    def _():
        w1_copy(7, w1_to[-1]).wait_send()

    def drain(kk, carry):
        k = column_of(kk)[0]
        for i in range(1, 8):
            w2_copy(kk, i).wait_send()
        for j in range(PIECES):
            @pl.when(base + 4 * k + j % 4 != f)
            def _():
                on_copy(kk, j % 4, j // 4, sib).wait_send()
        return carry

    lax.fori_loop(0, 2, drain, 0)


def write_out(all_ref, *refs):
    outs, sems = refs[:6], refs[6]
    copies = [
        pltpu.make_async_copy(all_ref.at[i], o.at[(0, 0) if i < 3 else (0,)], sems.at[i]) for i, o in enumerate(outs)
    ]
    for c in copies:
        c.start()
    for c in copies:
        c.wait()


def per_device(x_in, d_out, gate_weight, up_weight, down_weight, mom_gate, mom_up, mom_down, band_index):
    dma = pltpu.SemaphoreType.DMA
    block = (SIDE, SIDE)
    scratch = [
        pltpu.VMEM((2, 8 * SIDE, WIDE), BF16),
        pltpu.VMEM((3,) + block, BF16),
        pltpu.VMEM((2, 8, 4, 3, 16, SIDE), BF16),
        pltpu.VMEM((2, 4, 3) + block, F32),
        pltpu.VMEM((2, 4, 3) + block, BF16),
        pltpu.VMEM((2, 4, 3) + block, BF16),
        pltpu.VMEM((3, 3) + block, BF16),
        pltpu.VMEM((3,) + block, F32),
        pltpu.VMEM((3, 1, KEEP), jnp.int32),
        pltpu.VMEM((4,) + block, BF16),
        pltpu.VMEM((3, SIDE, KEEP), BF16),
        pltpu.VMEM((3, SIDE, KEEP), BF16),
        pltpu.VMEM((3,) + block, F32),
        pltpu.VMEM((16, SIDE), F32),
        pltpu.VMEM((8, 16, SIDE), F32),
        dma((10,)),
        dma((17,)),
        dma((17,)),
        dma((8,)),
        dma((2, 4)),
        dma((2, 8)),
        dma((2, 8)),
        dma((2, 4, 3)),
        dma((2, 4, 3)),
        dma((3, 3)),
        dma((8,)),
        dma((8,)),
    ]
    hbm = pl.BlockSpec(memory_space=pltpu.HBM)
    vmem = pl.BlockSpec(memory_space=pltpu.VMEM)
    results = pl.pallas_call(
        kernel,
        out_shape=jax.ShapeDtypeStruct((6,) + block, F32),
        in_specs=[hbm] * 10,
        out_specs=vmem,
        scratch_shapes=scratch,
        compiler_params=pltpu.CompilerParams(
            collective_id=0, has_side_effects=True, vmem_limit_bytes=62 * 1024 * 1024
        ),
        cost_estimate=pl.CostEstimate(flops=1700000000, bytes_accessed=2000000, transcendentals=300000),
    )(
        x_in, d_out, gate_weight, up_weight, down_weight, mom_gate, mom_up, mom_down, band_index,
        jnp.asarray(dct_parts()),
    )
    outs = [jax.ShapeDtypeStruct((1, 1) + block, F32)] * 3 + [jax.ShapeDtypeStruct((1,) + block, F32)] * 3
    return pl.pallas_call(
        write_out, out_shape=outs, in_specs=[vmem], out_specs=[hbm] * 6, scratch_shapes=[dma((6,))]
    )(results)


def solution(mesh):
    tokens = P("rep", "fsdp", None)
    weights = P("fsdp", None, None)
    moments = P("rep", "fsdp", None, None)
    return jax.shard_map(
        per_device, mesh=mesh,
        in_specs=(tokens, tokens, weights, weights, weights, moments, moments, moments, P(None, "fsdp", None)),
        out_specs=(moments, moments, moments, weights, weights, weights),
        check_vma=False,
    )
```

```python
import jax
import jax.numpy as jnp
import numpy as np
from jax import lax
from jax.experimental import pallas as pl
from jax.experimental.pallas import tpu as pltpu
from jax.sharding import PartitionSpec as P

MESH = pl.DeviceIdType.MESH
F32 = jnp.float32
BF16 = jnp.bfloat16
SIDE = 128
WIDE = 512
KEEP = 512
NZ = 16
HALF = SIDE // 2
PIECES = 12


def dct_parts():
    k = np.arange(SIDE, dtype=np.float64)[:, None]
    n = np.arange(SIDE, dtype=np.float64)[None, :]
    s = np.where(k == 0, np.sqrt(1.0 / SIDE), np.sqrt(2.0 / SIDE))
    c = (s * np.cos(np.pi * (2.0 * n + 1.0) * k / (2.0 * SIDE))).astype(np.float32)
    out = []
    for t in (c, c.T):
        hi = t.astype(jnp.bfloat16)
        lo = (t - hi.astype(np.float32)).astype(jnp.bfloat16)
        out += [hi, lo]
    return np.stack(out)


def mm(a, b, dims):
    return lax.dot_general(a, b, (dims, ((), ())), preferred_element_type=F32)


NN = ((1,), (0,))
NT = ((1,), (1,))
TN = ((0,), (0,))


def split(a):
    hi = a.astype(BF16)
    return hi, (a - hi.astype(F32)).astype(BF16)


def mm3(a, b, dims):
    return mm(a[0], b[0], dims) + (mm(a[0], b[1], dims) + mm(a[1], b[0], dims))


def kernel(
    x_ref, d_ref, wg_ref, wu_ref, wd_ref, mg_ref, mu_ref, md_ref, band_ref, table_ref,
    out,
    tok, mine_w, wts, part, recv, send, fin, mom, band, table, pick_r, pick_c, mask, vals, vals_all,
    load_sem, tok_send, tok_recv, w1_send, w1_recv, w2_send, w2_recv, rs_send, rs_recv, fin_recv,
    rep_send, rep_recv,
):
    f = lax.axis_index("fsdp")
    r = lax.axis_index("rep")
    core = f % 2
    z = (f // 2) % NZ
    xh = f // (2 * NZ)
    base = xh * (2 * NZ)
    sib = f + 1 - 2 * core
    partner = f + (1 - 2 * xh) * (2 * NZ)
    m_own = z // 2
    p_own = z % 2

    def chip(zz, c):
        return base + ((zz + NZ) % NZ) * 2 + c

    def remote(src, dst, ssem, rsem, target):
        return pltpu.make_async_remote_copy(
            src_ref=src, dst_ref=dst, send_sem=ssem, recv_sem=rsem,
            device_id={"fsdp": target}, device_id_type=MESH,
        )

    def to_rep(src, dst, ssem, rsem, target):
        return pltpu.make_async_remote_copy(
            src_ref=src, dst_ref=dst, send_sem=ssem, recv_sem=rsem,
            device_id={"rep": target}, device_id_type=MESH,
        )

    k_own = z // 2
    h_own = (k_own // 2) % 2
    kk_own = k_own // 4
    rb_own = f % 4
    skew = jnp.where(p_own == k_own % 2, 0, 1)
    w1_to = [chip(z + hop + skew, h_own) for hop in (8, -6, 6, -4, 4, -2, 2, 0)]
    w1_self = w1_to[-1] == f

    recv[...] = jnp.zeros(recv.shape, BF16)
    barrier = pltpu.get_barrier_semaphore()

    def greet(**to):
        pl.semaphore_signal(barrier, inc=1, device_id=to, device_id_type=MESH)

    sources = [base + 4 * (p_own + 2 * core + 4 * kk) + rb for kk in (0, 1) for rb in range(4)]
    for target in w1_to[:-1]:
        greet(fsdp=target)
    for source in sources + [w1_to[-1]]:
        @pl.when(source != f)
        def _():
            greet(fsdp=source)
    near = [chip(z + 2, core), chip(z - 2, core), chip(z + 1, core), chip(z - 1, core), partner, sib]
    for target in near:
        greet(fsdp=target)
    for i in range(1, 8):
        greet(rep=(r + i) % 8)

    slot = pl.multiple_of((2 * xh + core) * 2 * SIDE, 2 * SIDE)
    other = pl.multiple_of((2 * (1 - xh) + core) * 2 * SIDE, 2 * SIDE)
    loads = [
        pltpu.make_async_copy(band_ref, band, load_sem.at[0]),
        pltpu.make_async_copy(wg_ref.at[0], mine_w.at[0], load_sem.at[1]),
        pltpu.make_async_copy(wu_ref.at[0], mine_w.at[1], load_sem.at[2]),
        pltpu.make_async_copy(wd_ref.at[0], mine_w.at[2], load_sem.at[3]),
        pltpu.make_async_copy(x_ref.at[0], tok.at[0, pl.ds(slot, SIDE)], load_sem.at[4]),
        pltpu.make_async_copy(d_ref.at[0], tok.at[1, pl.ds(slot, SIDE)], load_sem.at[5]),
        pltpu.make_async_copy(mg_ref.at[0, 0], mom.at[0], load_sem.at[6]),
        pltpu.make_async_copy(mu_ref.at[0, 0], mom.at[1], load_sem.at[7]),
        pltpu.make_async_copy(md_ref.at[0, 0], mom.at[2], load_sem.at[8]),
        pltpu.make_async_copy(table_ref, table, load_sem.at[9]),
    ]
    for c in loads:
        c.start()

    vals[...] = jnp.zeros(vals.shape, F32)
    loads[0].wait()
    spots = lax.broadcasted_iota(jnp.int32, (SIDE, KEEP), 0)
    for m in range(3):
        at = band[m]
        pick_r[m] = jnp.where(spots == lax.shift_right_logical(at, 7), 1.0, 0.0).astype(BF16)
        pick_c[m] = jnp.where(spots == lax.bitwise_and(at, 127), 1.0, 0.0).astype(BF16)
    for m in range(3):
        mask[m] = mm(pick_c[m], pick_r[m], NT)
    for c in loads[1:]:
        c.wait()

    eighth = pl.ds(pl.multiple_of(r * 16, 16), 16)

    def w1_copy(i, target):
        return remote(
            mine_w.at[:, eighth], wts.at[kk_own, r, rb_own], w1_send.at[i], w1_recv.at[kk_own, rb_own], target
        )

    @pl.when(w1_self)
    def _():
        wts[kk_own, r, rb_own] = mine_w[:, eighth, :]

    pl.semaphore_wait(barrier, jnp.where(w1_self, 27, 29))

    for i, target in enumerate(w1_to[:-1]):
        w1_copy(i, target).start()

    @pl.when(jnp.logical_not(w1_self))
    def _():
        w1_copy(7, w1_to[-1]).start()

    def rows(start, size):
        return tok.at[:, pl.ds(start, size)]

    def tok_copy(i, src, dst, size, target):
        return remote(rows(src, size), rows(dst, size), tok_send.at[i], tok_recv.at[i], target)

    up = chip(z + 1, core)
    down = chip(z - 1, core)
    quarter = HALF // 2
    parts = [(0, up, SIDE), (HALF, down, SIDE), (quarter, up, SIDE), (HALF + quarter, down, SIDE)]
    to_partner = [tok_copy(i, slot + at, slot + at, quarter, partner) for i, (at, _, _) in enumerate(parts)]
    from_partner = [tok_copy(i, slot + at, other + at, quarter, partner) for i, (at, _, _) in enumerate(parts)]
    pass_near = [tok_copy(4 + i, other + at, other + at + off, quarter, to) for i, (at, to, off) in enumerate(parts)]
    pass_far = [tok_copy(8 + i, other + at + off, other + at + off, quarter, sib) for i, (at, _, off) in enumerate(parts)]
    to_up = tok_copy(12, slot, slot + SIDE, HALF, up)
    to_down = tok_copy(13, slot + HALF, slot + SIDE + HALF, HALF, down)
    to_sib = tok_copy(14, slot, slot, SIDE, sib)
    on_sib = tok_copy(15, other, other, SIDE, sib)
    near_sib = tok_copy(16, slot + SIDE, slot + SIDE, SIDE, sib)
    for c in to_partner + [to_up, to_down, to_sib]:
        c.start()

    def column_of(kk):
        k = p_own + 2 * core + 4 * kk
        ahead = (k - m_own + 8) % 8
        return k, ahead, jnp.where(ahead > 4, ahead - 4, 4 - ahead)

    stage_0 = column_of(0)[2]
    stage_1 = column_of(1)[2]
    first = jnp.where(stage_0 <= stage_1, 0, 1)

    def w2_copy(kk, i):
        piece = wts.at[kk, r]
        return to_rep(piece, piece, w2_send.at[kk, i], w2_recv.at[kk, r], (r + i) % 8)

    def w1_arrived(kk):
        k = column_of(kk)[0]
        for rb in range(4):
            @pl.when(base + 4 * k + rb != f)
            def _():
                remote(
                    mine_w.at[:, eighth], wts.at[kk, r, rb], w1_send.at[0], w1_recv.at[kk, rb], sib
                ).wait_recv()
        for i in range(1, 8):
            w2_copy(kk, i).start()

    def tokens_in(i):
        from_partner[i].wait_recv()
        pass_near[i].start()

    for i in range(4):
        tokens_in(i)
    on_sib.start()
    to_up.wait_recv()
    to_down.wait_recv()
    near_sib.start()
    w1_arrived(first)
    w1_arrived(1 - first)
    for c, d in zip(pass_near, pass_far):
        c.wait_recv()
        d.start()
    for c in [to_sib, on_sib, near_sib] + pass_far:
        c.wait_recv()

    def column(kk):
        xs = tok[0]
        ds = tok[1]
        w_g, w_u, w_d = ([wts[kk, :, i, m].reshape(SIDE, SIDE) for i in range(4)] for m in range(3))
        w_gu = jnp.concatenate([jnp.concatenate(w_g, axis=0), jnp.concatenate(w_u, axis=0)], axis=1)
        w_d = jnp.concatenate(w_d, axis=1)
        gu = mm(xs, w_gu, NN)
        dh = mm(ds, w_d, NT)
        gate = gu[:, :SIDE]
        upp = gu[:, SIDE:]
        sg = jax.nn.sigmoid(gate)
        act = gate * sg
        hidden = (act * upp).astype(BF16)
        d_gate = (dh * upp * sg * (1.0 + gate * (1.0 - sg))).astype(BF16)
        d_up = (dh * act).astype(BF16)
        g_in = mm(xs, jnp.concatenate([d_gate, d_up], axis=1), TN)
        g_out = mm(hidden, ds, TN)
        for i in range(4):
            part[kk, i, 0] = g_in[i * SIDE:(i + 1) * SIDE, :SIDE]
            part[kk, i, 1] = g_in[i * SIDE:(i + 1) * SIDE, SIDE:]
            part[kk, i, 2] = g_out[:, i * SIDE:(i + 1) * SIDE]

    def on_copy(kk, rb, m, target):
        return remote(send.at[kk, rb, m], recv.at[kk, rb, m], rs_send.at[kk, rb, m], rs_recv.at[kk, rb, m], target)

    def fin_copy(kk, rb, m, way, target):
        return remote(send.at[kk, rb, m], fin.at[way, m], rs_send.at[kk, rb, m], fin_recv.at[way, m], target)

    def turn_of(ahead, half):
        up_turn = 4 - half - ahead
        down_turn = ahead - 5 + half
        return jnp.where(ahead == 0, 2, jnp.where(ahead < 4, up_turn, jnp.where(ahead == 4, 0, down_turn)))

    def pass_on(kk, half, j):
        m = j // 2
        rb = 2 * half + j % 2
        k, ahead, stage = column_of(kk)
        heard = (turn_of(ahead, half) > 0) & (ahead != 0)
        upward = (ahead < 4) | ((ahead == 4) & (half == 0))
        last = (ahead == 0) | (ahead == 1) | (ahead == 7)
        owner = base + 4 * k + rb

        @pl.when(heard)
        def _():
            on_copy(kk, rb, m, sib).wait_recv()
        value = (part[kk, rb, m] + recv[kk, rb, m].astype(F32)).astype(BF16)
        send[kk, rb, m] = value

        @pl.when(jnp.logical_not(last))
        def _():
            on_copy(kk, rb, m, jnp.where(upward, chip(z + 2, core), chip(z - 2, core))).start()

        @pl.when(last & (owner != f))
        def _():
            way = jnp.where(ahead == 0, 2, jnp.where(ahead == 1, 0, 1))
            fin_copy(kk, rb, m, way, owner).start()

        @pl.when(last & (owner == f))
        def _():
            fin[2, m] = value

    def pass_turn(kks, turn):
        halves = [(kk, half) for kk in kks for half in (0, 1)]
        due = [turn_of(column_of(kk)[1], half) == turn for kk, half in halves]

        def step(j, carry):
            for (kk, half), now in zip(halves, due):
                @pl.when(now)
                def _():
                    pass_on(kk, half, j)
            return carry

        lax.fori_loop(0, PIECES // 2, step, 0)

    def work(i, carry):
        kk = jnp.where(i == 0, first, 1 - first)
        for q in range(1, 8):
            w2_in = wts.at[kk, (r + q) % 8]
            to_rep(w2_in, w2_in, w2_send.at[kk, q], w2_recv.at[kk, (r + q) % 8], r).wait_recv()
        column(kk)

        pass_turn((kk,), 0)
        return carry

    lax.fori_loop(0, 2, work, 0)

    def pass_rest(turn, carry):
        pass_turn((first, 1 - first), turn)
        return carry

    lax.fori_loop(1, 5, pass_rest, 0)

    c_m = (table[0], table[1])
    ct_m = (table[2], table[3])
    is_middle = (m_own == k_own) & (p_own == k_own % 2) & (core == h_own)
    moments = []
    coeffs = []
    for m in range(3):
        for way in (0, 1):
            fin_copy(0, 0, m, way, sib).wait_recv()

        @pl.when(jnp.logical_not(is_middle))
        def _():
            fin_copy(0, 0, m, 2, sib).wait_recv()
        total = fin[0, m].astype(F32) + fin[1, m].astype(F32) + fin[2, m].astype(F32)
        moment = 0.999 * mom[m] + total
        moments.append(moment)
        inner = mm3(c_m, split(moment), NN)
        coeff_t = mm3(c_m, split(inner), NT)
        coeffs.append(coeff_t)
        hi, lo = split(coeff_t)
        picked = mm(hi, pick_r[m], NN) + mm(lo, pick_r[m], NN)
        band_row = jnp.sum(picked * pick_c[m].astype(F32), axis=0, keepdims=True)
        for q in range(4):
            vals[4 * m + q:4 * m + q + 1, :] = band_row[:, q * SIDE:(q + 1) * SIDE]
    rep_copies = [to_rep(vals, vals_all.at[r], rep_send.at[i], rep_recv.at[r], (r + i) % 8) for i in range(1, 8)]
    for c in rep_copies:
        c.start()
    vals_all[r] = vals[...]

    for m in range(3):
        placed = jnp.where(mask[m] > 0.5, coeffs[m], 0.0)
        half = mm3(ct_m, split(placed), NT)
        out[m] = moments[m] - mm3(split(half), c_m, NN)

    for i in range(1, 8):
        q = (r + i) % 8
        to_rep(vals, vals_all.at[q], rep_send.at[i], rep_recv.at[q], q).wait_recv()
    summed = vals_all[0]
    for i in range(1, 8):
        summed = summed + vals_all[i]
    for m in range(3):
        hi, lo = split(jnp.concatenate([summed[4 * m + q:4 * m + q + 1, :] for q in range(4)], axis=1))
        cols = pick_c[m].astype(F32)
        placed = mm((cols * hi.astype(F32)).astype(BF16), pick_r[m], NT) + mm(
            (cols * lo.astype(F32)).astype(BF16), pick_r[m], NT
        )
        half = mm3(ct_m, split(placed), NT)
        out[3 + m] = mm3(split(half), c_m, NN)

    for c in to_partner + pass_near + pass_far + [to_up, to_down, to_sib, on_sib, near_sib]:
        c.wait_send()
    for c in rep_copies:
        c.wait_send()
    for i, target in enumerate(w1_to[:-1]):
        w1_copy(i, target).wait_send()

    @pl.when(jnp.logical_not(w1_self))
    def _():
        w1_copy(7, w1_to[-1]).wait_send()

    def drain(kk, carry):
        k = column_of(kk)[0]
        for i in range(1, 8):
            w2_copy(kk, i).wait_send()
        for j in range(PIECES):
            @pl.when(base + 4 * k + j % 4 != f)
            def _():
                on_copy(kk, j % 4, j // 4, sib).wait_send()
        return carry

    lax.fori_loop(0, 2, drain, 0)


def write_out(all_ref, *refs):
    outs, sems = refs[:6], refs[6]
    copies = [
        pltpu.make_async_copy(all_ref.at[i], o.at[(0, 0) if i < 3 else (0,)], sems.at[i]) for i, o in enumerate(outs)
    ]
    for c in copies:
        c.start()
    for c in copies:
        c.wait()


def per_device(x_in, d_out, gate_weight, up_weight, down_weight, mom_gate, mom_up, mom_down, band_index):
    dma = pltpu.SemaphoreType.DMA
    block = (SIDE, SIDE)
    scratch = [
        pltpu.VMEM((2, 8 * SIDE, WIDE), BF16),
        pltpu.VMEM((3,) + block, BF16),
        pltpu.VMEM((2, 8, 4, 3, 16, SIDE), BF16),
        pltpu.VMEM((2, 4, 3) + block, F32),
        pltpu.VMEM((2, 4, 3) + block, BF16),
        pltpu.VMEM((2, 4, 3) + block, BF16),
        pltpu.VMEM((3, 3) + block, BF16),
        pltpu.VMEM((3,) + block, F32),
        pltpu.VMEM((3, 1, KEEP), jnp.int32),
        pltpu.VMEM((4,) + block, BF16),
        pltpu.VMEM((3, SIDE, KEEP), BF16),
        pltpu.VMEM((3, SIDE, KEEP), BF16),
        pltpu.VMEM((3,) + block, F32),
        pltpu.VMEM((16, SIDE), F32),
        pltpu.VMEM((8, 16, SIDE), F32),
        dma((10,)),
        dma((17,)),
        dma((17,)),
        dma((8,)),
        dma((2, 4)),
        dma((2, 8)),
        dma((2, 8)),
        dma((2, 4, 3)),
        dma((2, 4, 3)),
        dma((3, 3)),
        dma((8,)),
        dma((8,)),
    ]
    hbm = pl.BlockSpec(memory_space=pltpu.HBM)
    vmem = pl.BlockSpec(memory_space=pltpu.VMEM)
    results = pl.pallas_call(
        kernel,
        out_shape=jax.ShapeDtypeStruct((6,) + block, F32),
        in_specs=[hbm] * 10,
        out_specs=vmem,
        scratch_shapes=scratch,
        compiler_params=pltpu.CompilerParams(
            collective_id=0, has_side_effects=True, vmem_limit_bytes=62 * 1024 * 1024
        ),
        cost_estimate=pl.CostEstimate(flops=1700000000, bytes_accessed=2000000, transcendentals=300000),
    )(
        x_in, d_out, gate_weight, up_weight, down_weight, mom_gate, mom_up, mom_down, band_index,
        jnp.asarray(dct_parts()),
    )
    outs = [jax.ShapeDtypeStruct((1, 1) + block, F32)] * 3 + [jax.ShapeDtypeStruct((1,) + block, F32)] * 3
    return pl.pallas_call(
        write_out, out_shape=outs, in_specs=[vmem], out_specs=[hbm] * 6, scratch_shapes=[dma((6,))]
    )(results)


def solution(mesh):
    tokens = P("rep", "fsdp", None)
    weights = P("fsdp", None, None)
    moments = P("rep", "fsdp", None, None)
    return jax.shard_map(
        per_device, mesh=mesh,
        in_specs=(tokens, tokens, weights, weights, weights, moments, moments, moments, P(None, "fsdp", None)),
        out_specs=(moments, moments, moments, weights, weights, weights),
        check_vma=False,
    )
```

```python
import jax
import jax.numpy as jnp
import numpy as np
from jax import lax
from jax.experimental import pallas as pl
from jax.experimental.pallas import tpu as pltpu
from jax.sharding import PartitionSpec as P

MESH = pl.DeviceIdType.MESH
F32 = jnp.float32
BF16 = jnp.bfloat16
SIDE = 128
WIDE = 512
KEEP = 512
NZ = 16
HALF = SIDE // 2
PIECES = 12


def dct_parts():
    k = np.arange(SIDE, dtype=np.float64)[:, None]
    n = np.arange(SIDE, dtype=np.float64)[None, :]
    s = np.where(k == 0, np.sqrt(1.0 / SIDE), np.sqrt(2.0 / SIDE))
    c = (s * np.cos(np.pi * (2.0 * n + 1.0) * k / (2.0 * SIDE))).astype(np.float32)
    out = []
    for t in (c, c.T):
        hi = t.astype(jnp.bfloat16)
        lo = (t - hi.astype(np.float32)).astype(jnp.bfloat16)
        out += [hi, lo]
    return np.stack(out)


def mm(a, b, dims):
    return lax.dot_general(a, b, (dims, ((), ())), preferred_element_type=F32)


NN = ((1,), (0,))
NT = ((1,), (1,))
TN = ((0,), (0,))


def split(a):
    hi = a.astype(BF16)
    return hi, (a - hi.astype(F32)).astype(BF16)


def mm3(a, b, dims):
    return mm(a[0], b[0], dims) + (mm(a[0], b[1], dims) + mm(a[1], b[0], dims))


def kernel(
    x_ref, d_ref, wg_ref, wu_ref, wd_ref, mg_ref, mu_ref, md_ref, band_ref, table_ref,
    out,
    tok, mine_w, wts, part, recv, send, fin, mom, band, table, pick_r, pick_c, mask, vals, vals_all,
    load_sem, tok_send, tok_recv, w1_send, w1_recv, w2_send, w2_recv, rs_send, rs_recv, fin_recv,
    rep_send, rep_recv,
):
    f = lax.axis_index("fsdp")
    r = lax.axis_index("rep")
    core = f % 2
    z = (f // 2) % NZ
    xh = f // (2 * NZ)
    base = xh * (2 * NZ)
    sib = f + 1 - 2 * core
    partner = f + (1 - 2 * xh) * (2 * NZ)
    m_own = z // 2
    p_own = z % 2

    def chip(zz, c):
        return base + ((zz + NZ) % NZ) * 2 + c

    def remote(src, dst, ssem, rsem, target):
        return pltpu.make_async_remote_copy(
            src_ref=src, dst_ref=dst, send_sem=ssem, recv_sem=rsem,
            device_id={"fsdp": target}, device_id_type=MESH,
        )

    def to_rep(src, dst, ssem, rsem, target):
        return pltpu.make_async_remote_copy(
            src_ref=src, dst_ref=dst, send_sem=ssem, recv_sem=rsem,
            device_id={"rep": target}, device_id_type=MESH,
        )

    k_own = z // 2
    h_own = (k_own // 2) % 2
    kk_own = k_own // 4
    rb_own = f % 4
    skew = jnp.where(p_own == k_own % 2, 0, 1)
    w1_to = [chip(z + hop + skew, h_own) for hop in (8, 6, -6, 4, -4, 2, -2, 0)]
    w1_self = w1_to[-1] == f

    recv[...] = jnp.zeros(recv.shape, BF16)
    barrier = pltpu.get_barrier_semaphore()

    def greet(**to):
        pl.semaphore_signal(barrier, inc=1, device_id=to, device_id_type=MESH)

    sources = [base + 4 * (p_own + 2 * core + 4 * kk) + rb for kk in (0, 1) for rb in range(4)]
    for target in w1_to[:-1]:
        greet(fsdp=target)
    for source in sources + [w1_to[-1]]:
        @pl.when(source != f)
        def _():
            greet(fsdp=source)
    near = [chip(z + 2, core), chip(z - 2, core), chip(z + 1, core), chip(z - 1, core), partner, sib]
    for target in near:
        greet(fsdp=target)
    for i in range(1, 8):
        greet(rep=(r + i) % 8)

    slot = pl.multiple_of((2 * xh + core) * 2 * SIDE, 2 * SIDE)
    other = pl.multiple_of((2 * (1 - xh) + core) * 2 * SIDE, 2 * SIDE)
    loads = [
        pltpu.make_async_copy(band_ref, band, load_sem.at[0]),
        pltpu.make_async_copy(wg_ref.at[0], mine_w.at[0], load_sem.at[1]),
        pltpu.make_async_copy(wu_ref.at[0], mine_w.at[1], load_sem.at[2]),
        pltpu.make_async_copy(wd_ref.at[0], mine_w.at[2], load_sem.at[3]),
        pltpu.make_async_copy(x_ref.at[0], tok.at[0, pl.ds(slot, SIDE)], load_sem.at[4]),
        pltpu.make_async_copy(d_ref.at[0], tok.at[1, pl.ds(slot, SIDE)], load_sem.at[5]),
        pltpu.make_async_copy(mg_ref.at[0, 0], mom.at[0], load_sem.at[6]),
        pltpu.make_async_copy(mu_ref.at[0, 0], mom.at[1], load_sem.at[7]),
        pltpu.make_async_copy(md_ref.at[0, 0], mom.at[2], load_sem.at[8]),
        pltpu.make_async_copy(table_ref, table, load_sem.at[9]),
    ]
    for c in loads:
        c.start()

    vals[...] = jnp.zeros(vals.shape, F32)
    loads[0].wait()
    spots = lax.broadcasted_iota(jnp.int32, (SIDE, KEEP), 0)
    for m in range(3):
        at = band[m]
        pick_r[m] = jnp.where(spots == lax.shift_right_logical(at, 7), 1.0, 0.0).astype(BF16)
        pick_c[m] = jnp.where(spots == lax.bitwise_and(at, 127), 1.0, 0.0).astype(BF16)
    for m in range(3):
        mask[m] = mm(pick_c[m], pick_r[m], NT)
    for c in loads[1:]:
        c.wait()

    eighth = pl.ds(pl.multiple_of(r * 16, 16), 16)

    def w1_copy(i, target):
        return remote(
            mine_w.at[:, eighth], wts.at[kk_own, r, rb_own], w1_send.at[i], w1_recv.at[kk_own, rb_own], target
        )

    @pl.when(w1_self)
    def _():
        wts[kk_own, r, rb_own] = mine_w[:, eighth, :]

    pl.semaphore_wait(barrier, jnp.where(w1_self, 27, 29))

    for i, target in enumerate(w1_to[:-1]):
        w1_copy(i, target).start()

    @pl.when(jnp.logical_not(w1_self))
    def _():
        w1_copy(7, w1_to[-1]).start()

    def rows(start, size):
        return tok.at[:, pl.ds(start, size)]

    def tok_copy(i, src, dst, size, target):
        return remote(rows(src, size), rows(dst, size), tok_send.at[i], tok_recv.at[i], target)

    up = chip(z + 1, core)
    down = chip(z - 1, core)
    quarter = HALF // 2
    parts = [(0, up, SIDE), (HALF, down, SIDE), (quarter, up, SIDE), (HALF + quarter, down, SIDE)]
    to_partner = [tok_copy(i, slot + at, slot + at, quarter, partner) for i, (at, _, _) in enumerate(parts)]
    from_partner = [tok_copy(i, slot + at, other + at, quarter, partner) for i, (at, _, _) in enumerate(parts)]
    pass_near = [tok_copy(4 + i, other + at, other + at + off, quarter, to) for i, (at, to, off) in enumerate(parts)]
    pass_far = [tok_copy(8 + i, other + at + off, other + at + off, quarter, sib) for i, (at, _, off) in enumerate(parts)]
    to_up = tok_copy(12, slot, slot + SIDE, HALF, up)
    to_down = tok_copy(13, slot + HALF, slot + SIDE + HALF, HALF, down)
    to_sib = tok_copy(14, slot, slot, SIDE, sib)
    on_sib = tok_copy(15, other, other, SIDE, sib)
    near_sib = tok_copy(16, slot + SIDE, slot + SIDE, SIDE, sib)
    for c in to_partner + [to_sib]:
        c.start()

    def column_of(kk):
        k = p_own + 2 * core + 4 * kk
        ahead = (k - m_own + 8) % 8
        return k, ahead, jnp.where(ahead > 4, ahead - 4, 4 - ahead)

    stage_0 = column_of(0)[2]
    stage_1 = column_of(1)[2]
    first = jnp.where(stage_0 <= stage_1, 0, 1)

    def w2_copy(kk, i):
        piece = wts.at[kk, r]
        return to_rep(piece, piece, w2_send.at[kk, i], w2_recv.at[kk, r], (r + i) % 8)

    def w1_arrived(kk):
        k = column_of(kk)[0]
        for rb in range(4):
            @pl.when(base + 4 * k + rb != f)
            def _():
                remote(
                    mine_w.at[:, eighth], wts.at[kk, r, rb], w1_send.at[0], w1_recv.at[kk, rb], sib
                ).wait_recv()
        for i in range(1, 8):
            w2_copy(kk, i).start()

    def tokens_in(i):
        from_partner[i].wait_recv()
        pass_near[i].start()

    for i in range(4):
        tokens_in(i)
    to_up.start()
    to_down.start()
    on_sib.start()
    w1_arrived(first)
    w1_arrived(1 - first)
    to_up.wait_recv()
    to_down.wait_recv()
    near_sib.start()
    for c, d in zip(pass_near, pass_far):
        c.wait_recv()
        d.start()
    for c in [to_sib, on_sib, near_sib] + pass_far:
        c.wait_recv()

    def column(kk):
        xs = tok[0]
        ds = tok[1]
        w_g, w_u, w_d = ([wts[kk, :, i, m].reshape(SIDE, SIDE) for i in range(4)] for m in range(3))
        w_gu = jnp.concatenate([jnp.concatenate(w_g, axis=0), jnp.concatenate(w_u, axis=0)], axis=1)
        w_d = jnp.concatenate(w_d, axis=1)
        gu = mm(xs, w_gu, NN)
        dh = mm(ds, w_d, NT)
        gate = gu[:, :SIDE]
        upp = gu[:, SIDE:]
        sg = jax.nn.sigmoid(gate)
        act = gate * sg
        hidden = (act * upp).astype(BF16)
        d_gate = (dh * upp * sg * (1.0 + gate * (1.0 - sg))).astype(BF16)
        d_up = (dh * act).astype(BF16)
        g_in = mm(xs, jnp.concatenate([d_gate, d_up], axis=1), TN)
        g_out = mm(hidden, ds, TN)
        for i in range(4):
            part[kk, i, 0] = g_in[i * SIDE:(i + 1) * SIDE, :SIDE]
            part[kk, i, 1] = g_in[i * SIDE:(i + 1) * SIDE, SIDE:]
            part[kk, i, 2] = g_out[:, i * SIDE:(i + 1) * SIDE]

    def on_copy(kk, rb, m, target):
        return remote(send.at[kk, rb, m], recv.at[kk, rb, m], rs_send.at[kk, rb, m], rs_recv.at[kk, rb, m], target)

    def fin_copy(kk, rb, m, way, target):
        return remote(send.at[kk, rb, m], fin.at[way, m], rs_send.at[kk, rb, m], fin_recv.at[way, m], target)

    def turn_of(ahead, half):
        up_turn = 4 - half - ahead
        down_turn = ahead - 5 + half
        return jnp.where(ahead == 0, 2, jnp.where(ahead < 4, up_turn, jnp.where(ahead == 4, 0, down_turn)))

    def pass_on(kk, half, j):
        m = j // 2
        rb = 2 * half + j % 2
        k, ahead, stage = column_of(kk)
        heard = (turn_of(ahead, half) > 0) & (ahead != 0)
        upward = (ahead < 4) | ((ahead == 4) & (half == 0))
        last = (ahead == 0) | (ahead == 1) | (ahead == 7)
        owner = base + 4 * k + rb

        @pl.when(heard)
        def _():
            on_copy(kk, rb, m, sib).wait_recv()
        value = (part[kk, rb, m] + recv[kk, rb, m].astype(F32)).astype(BF16)
        send[kk, rb, m] = value

        @pl.when(jnp.logical_not(last))
        def _():
            on_copy(kk, rb, m, jnp.where(upward, chip(z + 2, core), chip(z - 2, core))).start()

        @pl.when(last & (owner != f))
        def _():
            way = jnp.where(ahead == 0, 2, jnp.where(ahead == 1, 0, 1))
            fin_copy(kk, rb, m, way, owner).start()

        @pl.when(last & (owner == f))
        def _():
            fin[2, m] = value

    def pass_turn(kks, turn):
        halves = [(kk, half) for kk in kks for half in (0, 1)]
        due = [turn_of(column_of(kk)[1], half) == turn for kk, half in halves]

        def step(j, carry):
            for (kk, half), now in zip(halves, due):
                @pl.when(now)
                def _():
                    pass_on(kk, half, j)
            return carry

        lax.fori_loop(0, PIECES // 2, step, 0)

    def work(i, carry):
        kk = jnp.where(i == 0, first, 1 - first)
        for q in range(1, 8):
            w2_in = wts.at[kk, (r + q) % 8]
            to_rep(w2_in, w2_in, w2_send.at[kk, q], w2_recv.at[kk, (r + q) % 8], r).wait_recv()
        column(kk)

        pass_turn((kk,), 0)
        return carry

    lax.fori_loop(0, 2, work, 0)

    def pass_rest(turn, carry):
        pass_turn((first, 1 - first), turn)
        return carry

    lax.fori_loop(1, 5, pass_rest, 0)

    c_m = (table[0], table[1])
    ct_m = (table[2], table[3])
    is_middle = (m_own == k_own) & (p_own == k_own % 2) & (core == h_own)
    moments = []
    coeffs = []
    for m in range(3):
        for way in (0, 1):
            fin_copy(0, 0, m, way, sib).wait_recv()

        @pl.when(jnp.logical_not(is_middle))
        def _():
            fin_copy(0, 0, m, 2, sib).wait_recv()
        total = fin[0, m].astype(F32) + fin[1, m].astype(F32) + fin[2, m].astype(F32)
        moment = 0.999 * mom[m] + total
        moments.append(moment)
        inner = mm3(c_m, split(moment), NN)
        coeff_t = mm3(c_m, split(inner), NT)
        coeffs.append(coeff_t)
        hi, lo = split(coeff_t)
        picked = mm(hi, pick_r[m], NN) + mm(lo, pick_r[m], NN)
        band_row = jnp.sum(picked * pick_c[m].astype(F32), axis=0, keepdims=True)
        for q in range(4):
            vals[4 * m + q:4 * m + q + 1, :] = band_row[:, q * SIDE:(q + 1) * SIDE]
    rep_copies = [to_rep(vals, vals_all.at[r], rep_send.at[i], rep_recv.at[r], (r + i) % 8) for i in range(1, 8)]
    for c in rep_copies:
        c.start()
    vals_all[r] = vals[...]

    for m in range(3):
        placed = jnp.where(mask[m] > 0.5, coeffs[m], 0.0)
        half = mm3(ct_m, split(placed), NT)
        out[m] = moments[m] - mm3(split(half), c_m, NN)

    for i in range(1, 8):
        q = (r + i) % 8
        to_rep(vals, vals_all.at[q], rep_send.at[i], rep_recv.at[q], q).wait_recv()
    summed = vals_all[0]
    for i in range(1, 8):
        summed = summed + vals_all[i]
    for m in range(3):
        hi, lo = split(jnp.concatenate([summed[4 * m + q:4 * m + q + 1, :] for q in range(4)], axis=1))
        cols = pick_c[m].astype(F32)
        placed = mm((cols * hi.astype(F32)).astype(BF16), pick_r[m], NT) + mm(
            (cols * lo.astype(F32)).astype(BF16), pick_r[m], NT
        )
        half = mm3(ct_m, split(placed), NT)
        out[3 + m] = mm3(split(half), c_m, NN)

    for c in to_partner + pass_near + pass_far + [to_up, to_down, to_sib, on_sib, near_sib]:
        c.wait_send()
    for c in rep_copies:
        c.wait_send()
    for i, target in enumerate(w1_to[:-1]):
        w1_copy(i, target).wait_send()

    @pl.when(jnp.logical_not(w1_self))
    def _():
        w1_copy(7, w1_to[-1]).wait_send()

    def drain(kk, carry):
        k = column_of(kk)[0]
        for i in range(1, 8):
            w2_copy(kk, i).wait_send()
        for j in range(PIECES):
            @pl.when(base + 4 * k + j % 4 != f)
            def _():
                on_copy(kk, j % 4, j // 4, sib).wait_send()
        return carry

    lax.fori_loop(0, 2, drain, 0)


def write_out(all_ref, *refs):
    outs, sems = refs[:6], refs[6]
    copies = [
        pltpu.make_async_copy(all_ref.at[i], o.at[(0, 0) if i < 3 else (0,)], sems.at[i]) for i, o in enumerate(outs)
    ]
    for c in copies:
        c.start()
    for c in copies:
        c.wait()


def per_device(x_in, d_out, gate_weight, up_weight, down_weight, mom_gate, mom_up, mom_down, band_index):
    dma = pltpu.SemaphoreType.DMA
    block = (SIDE, SIDE)
    scratch = [
        pltpu.VMEM((2, 8 * SIDE, WIDE), BF16),
        pltpu.VMEM((3,) + block, BF16),
        pltpu.VMEM((2, 8, 4, 3, 16, SIDE), BF16),
        pltpu.VMEM((2, 4, 3) + block, F32),
        pltpu.VMEM((2, 4, 3) + block, BF16),
        pltpu.VMEM((2, 4, 3) + block, BF16),
        pltpu.VMEM((3, 3) + block, BF16),
        pltpu.VMEM((3,) + block, F32),
        pltpu.VMEM((3, 1, KEEP), jnp.int32),
        pltpu.VMEM((4,) + block, BF16),
        pltpu.VMEM((3, SIDE, KEEP), BF16),
        pltpu.VMEM((3, SIDE, KEEP), BF16),
        pltpu.VMEM((3,) + block, F32),
        pltpu.VMEM((16, SIDE), F32),
        pltpu.VMEM((8, 16, SIDE), F32),
        dma((10,)),
        dma((17,)),
        dma((17,)),
        dma((8,)),
        dma((2, 4)),
        dma((2, 8)),
        dma((2, 8)),
        dma((2, 4, 3)),
        dma((2, 4, 3)),
        dma((3, 3)),
        dma((8,)),
        dma((8,)),
    ]
    hbm = pl.BlockSpec(memory_space=pltpu.HBM)
    vmem = pl.BlockSpec(memory_space=pltpu.VMEM)
    results = pl.pallas_call(
        kernel,
        out_shape=jax.ShapeDtypeStruct((6,) + block, F32),
        in_specs=[hbm] * 10,
        out_specs=vmem,
        scratch_shapes=scratch,
        compiler_params=pltpu.CompilerParams(
            collective_id=0, has_side_effects=True, vmem_limit_bytes=62 * 1024 * 1024
        ),
        cost_estimate=pl.CostEstimate(flops=1700000000, bytes_accessed=2000000, transcendentals=300000),
    )(
        x_in, d_out, gate_weight, up_weight, down_weight, mom_gate, mom_up, mom_down, band_index,
        jnp.asarray(dct_parts()),
    )
    outs = [jax.ShapeDtypeStruct((1, 1) + block, F32)] * 3 + [jax.ShapeDtypeStruct((1,) + block, F32)] * 3
    return pl.pallas_call(
        write_out, out_shape=outs, in_specs=[vmem], out_specs=[hbm] * 6, scratch_shapes=[dma((6,))]
    )(results)


def solution(mesh):
    tokens = P("rep", "fsdp", None)
    weights = P("fsdp", None, None)
    moments = P("rep", "fsdp", None, None)
    return jax.shard_map(
        per_device, mesh=mesh,
        in_specs=(tokens, tokens, weights, weights, weights, moments, moments, moments, P(None, "fsdp", None)),
        out_specs=(moments, moments, moments, weights, weights, weights),
        check_vma=False,
    )
```

```python
import jax
import jax.numpy as jnp
import numpy as np
from jax import lax
from jax.experimental import pallas as pl
from jax.experimental.pallas import tpu as pltpu
from jax.sharding import PartitionSpec as P

MESH = pl.DeviceIdType.MESH
F32 = jnp.float32
BF16 = jnp.bfloat16
SIDE = 128
WIDE = 512
KEEP = 512
NZ = 16
HALF = SIDE // 2
PIECES = 12


def dct_parts():
    k = np.arange(SIDE, dtype=np.float64)[:, None]
    n = np.arange(SIDE, dtype=np.float64)[None, :]
    s = np.where(k == 0, np.sqrt(1.0 / SIDE), np.sqrt(2.0 / SIDE))
    c = (s * np.cos(np.pi * (2.0 * n + 1.0) * k / (2.0 * SIDE))).astype(np.float32)
    out = []
    for t in (c, c.T):
        hi = t.astype(jnp.bfloat16)
        lo = (t - hi.astype(np.float32)).astype(jnp.bfloat16)
        out += [hi, lo]
    return np.stack(out)


def mm(a, b, dims):
    return lax.dot_general(a, b, (dims, ((), ())), preferred_element_type=F32)


NN = ((1,), (0,))
NT = ((1,), (1,))
TN = ((0,), (0,))


def split(a):
    hi = a.astype(BF16)
    return hi, (a - hi.astype(F32)).astype(BF16)


def mm3(a, b, dims):
    return mm(a[0], b[0], dims) + (mm(a[0], b[1], dims) + mm(a[1], b[0], dims))


def kernel(
    x_ref, d_ref, wg_ref, wu_ref, wd_ref, mg_ref, mu_ref, md_ref, band_ref, table_ref,
    out,
    tok, mine_w, wts, part, recv, send, fin, mom, band, table, pick_r, pick_c, mask, vals, vals_all,
    load_sem, tok_send, tok_recv, w1_send, w1_recv, w2_send, w2_recv, rs_send, rs_recv, fin_recv,
    rep_send, rep_recv,
):
    f = lax.axis_index("fsdp")
    r = lax.axis_index("rep")
    core = f % 2
    z = (f // 2) % NZ
    xh = f // (2 * NZ)
    base = xh * (2 * NZ)
    sib = f + 1 - 2 * core
    partner = f + (1 - 2 * xh) * (2 * NZ)
    m_own = z // 2
    p_own = z % 2

    def chip(zz, c):
        return base + ((zz + NZ) % NZ) * 2 + c

    def remote(src, dst, ssem, rsem, target):
        return pltpu.make_async_remote_copy(
            src_ref=src, dst_ref=dst, send_sem=ssem, recv_sem=rsem,
            device_id={"fsdp": target}, device_id_type=MESH,
        )

    def to_rep(src, dst, ssem, rsem, target):
        return pltpu.make_async_remote_copy(
            src_ref=src, dst_ref=dst, send_sem=ssem, recv_sem=rsem,
            device_id={"rep": target}, device_id_type=MESH,
        )

    k_own = z // 2
    h_own = (k_own // 2) % 2
    kk_own = k_own // 4
    rb_own = f % 4
    skew = jnp.where(p_own == k_own % 2, 0, 1)
    w1_to = [chip(z + hop + skew, h_own) for hop in (8, 6, -6, 4, -4, 2, -2, 0)]
    w1_self = w1_to[-1] == f

    recv[...] = jnp.zeros(recv.shape, BF16)
    barrier = pltpu.get_barrier_semaphore()

    def greet(**to):
        pl.semaphore_signal(barrier, inc=1, device_id=to, device_id_type=MESH)

    sources = [base + 4 * (p_own + 2 * core + 4 * kk) + rb for kk in (0, 1) for rb in range(4)]
    for target in w1_to[:-1]:
        greet(fsdp=target)
    for source in sources + [w1_to[-1]]:
        @pl.when(source != f)
        def _():
            greet(fsdp=source)
    near = [chip(z + 2, core), chip(z - 2, core), chip(z + 1, core), chip(z - 1, core), partner, sib]
    for target in near:
        greet(fsdp=target)
    for i in range(1, 8):
        greet(rep=(r + i) % 8)

    slot = pl.multiple_of((2 * xh + core) * 2 * SIDE, 2 * SIDE)
    other = pl.multiple_of((2 * (1 - xh) + core) * 2 * SIDE, 2 * SIDE)
    loads = [
        pltpu.make_async_copy(band_ref, band, load_sem.at[0]),
        pltpu.make_async_copy(wg_ref.at[0], mine_w.at[0], load_sem.at[1]),
        pltpu.make_async_copy(wu_ref.at[0], mine_w.at[1], load_sem.at[2]),
        pltpu.make_async_copy(wd_ref.at[0], mine_w.at[2], load_sem.at[3]),
        pltpu.make_async_copy(x_ref.at[0], tok.at[0, pl.ds(slot, SIDE)], load_sem.at[4]),
        pltpu.make_async_copy(d_ref.at[0], tok.at[1, pl.ds(slot, SIDE)], load_sem.at[5]),
        pltpu.make_async_copy(mg_ref.at[0, 0], mom.at[0], load_sem.at[6]),
        pltpu.make_async_copy(mu_ref.at[0, 0], mom.at[1], load_sem.at[7]),
        pltpu.make_async_copy(md_ref.at[0, 0], mom.at[2], load_sem.at[8]),
        pltpu.make_async_copy(table_ref, table, load_sem.at[9]),
    ]
    for c in loads:
        c.start()

    vals[...] = jnp.zeros(vals.shape, F32)
    loads[0].wait()
    spots = lax.broadcasted_iota(jnp.int32, (SIDE, KEEP), 0)
    for m in range(3):
        at = band[m]
        pick_r[m] = jnp.where(spots == lax.shift_right_logical(at, 7), 1.0, 0.0).astype(BF16)
        pick_c[m] = jnp.where(spots == lax.bitwise_and(at, 127), 1.0, 0.0).astype(BF16)
    for m in range(3):
        mask[m] = mm(pick_c[m], pick_r[m], NT)
    for c in loads[1:]:
        c.wait()

    eighth = pl.ds(pl.multiple_of(r * 16, 16), 16)

    def w1_copy(i, target):
        return remote(
            mine_w.at[:, eighth], wts.at[kk_own, r, rb_own], w1_send.at[i], w1_recv.at[kk_own, rb_own], target
        )

    @pl.when(w1_self)
    def _():
        wts[kk_own, r, rb_own] = mine_w[:, eighth, :]

    pl.semaphore_wait(barrier, jnp.where(w1_self, 27, 29))

    for i, target in enumerate(w1_to[:-1]):
        w1_copy(i, target).start()

    @pl.when(jnp.logical_not(w1_self))
    def _():
        w1_copy(7, w1_to[-1]).start()

    def rows(start, size):
        return tok.at[:, pl.ds(start, size)]

    def tok_copy(i, src, dst, size, target):
        return remote(rows(src, size), rows(dst, size), tok_send.at[i], tok_recv.at[i], target)

    up = chip(z + 1, core)
    down = chip(z - 1, core)
    quarter = HALF // 2
    parts = [(0, up, SIDE), (HALF, down, SIDE), (quarter, up, SIDE), (HALF + quarter, down, SIDE)]
    to_partner = [tok_copy(i, slot + at, slot + at, quarter, partner) for i, (at, _, _) in enumerate(parts)]
    from_partner = [tok_copy(i, slot + at, other + at, quarter, partner) for i, (at, _, _) in enumerate(parts)]
    pass_near = [tok_copy(4 + i, other + at, other + at + off, quarter, to) for i, (at, to, off) in enumerate(parts)]
    pass_far = [tok_copy(8 + i, other + at + off, other + at + off, quarter, sib) for i, (at, _, off) in enumerate(parts)]
    to_up = tok_copy(12, slot, slot + SIDE, HALF, up)
    to_down = tok_copy(13, slot + HALF, slot + SIDE + HALF, HALF, down)
    to_sib = tok_copy(14, slot, slot, SIDE, sib)
    on_sib = tok_copy(15, other, other, SIDE, sib)
    near_sib = tok_copy(16, slot + SIDE, slot + SIDE, SIDE, sib)
    for c in to_partner + [to_up, to_down, to_sib]:
        c.start()

    def column_of(kk):
        k = p_own + 2 * core + 4 * kk
        ahead = (k - m_own + 8) % 8
        return k, ahead, jnp.where(ahead > 4, ahead - 4, 4 - ahead)

    stage_0 = column_of(0)[2]
    stage_1 = column_of(1)[2]
    first = jnp.where(stage_0 <= stage_1, 0, 1)

    def w2_copy(kk, i):
        piece = wts.at[kk, r]
        return to_rep(piece, piece, w2_send.at[kk, i], w2_recv.at[kk, r], (r + i) % 8)

    def w1_arrived(kk):
        k = column_of(kk)[0]
        for rb in range(4):
            @pl.when(base + 4 * k + rb != f)
            def _():
                remote(
                    mine_w.at[:, eighth], wts.at[kk, r, rb], w1_send.at[0], w1_recv.at[kk, rb], sib
                ).wait_recv()
        for i in range(1, 8):
            w2_copy(kk, i).start()

    def tokens_in(i):
        from_partner[i].wait_recv()
        pass_near[i].start()

    for i in range(4):
        tokens_in(i)
    on_sib.start()
    to_up.wait_recv()
    to_down.wait_recv()
    near_sib.start()
    w1_arrived(first)
    w1_arrived(1 - first)
    for c, d in zip(pass_near, pass_far):
        c.wait_recv()
        d.start()
    for c in [to_sib, on_sib, near_sib] + pass_far:
        c.wait_recv()

    def column(kk):
        xs = tok[0]
        ds = tok[1]
        w_g, w_u, w_d = ([wts[kk, :, i, m].reshape(SIDE, SIDE) for i in range(4)] for m in range(3))
        w_gu = jnp.concatenate([jnp.concatenate(w_g, axis=0), jnp.concatenate(w_u, axis=0)], axis=1)
        w_d = jnp.concatenate(w_d, axis=1)
        gu = mm(xs, w_gu, NN)
        dh = mm(ds, w_d, NT)
        gate = gu[:, :SIDE]
        upp = gu[:, SIDE:]
        sg = jax.nn.sigmoid(gate)
        act = gate * sg
        hidden = (act * upp).astype(BF16)
        d_gate = (dh * upp * sg * (1.0 + gate * (1.0 - sg))).astype(BF16)
        d_up = (dh * act).astype(BF16)
        g_in = mm(xs, jnp.concatenate([d_gate, d_up], axis=1), TN)
        g_out = mm(hidden, ds, TN)
        for i in range(4):
            part[kk, i, 0] = g_in[i * SIDE:(i + 1) * SIDE, :SIDE]
            part[kk, i, 1] = g_in[i * SIDE:(i + 1) * SIDE, SIDE:]
            part[kk, i, 2] = g_out[:, i * SIDE:(i + 1) * SIDE]

    def on_copy(kk, rb, m, target):
        return remote(send.at[kk, rb, m], recv.at[kk, rb, m], rs_send.at[kk, rb, m], rs_recv.at[kk, rb, m], target)

    def fin_copy(kk, rb, m, way, target):
        return remote(send.at[kk, rb, m], fin.at[way, m], rs_send.at[kk, rb, m], fin_recv.at[way, m], target)

    def turn_of(ahead, half):
        up_turn = 4 - half - ahead
        down_turn = ahead - 5 + half
        return jnp.where(ahead == 0, 2, jnp.where(ahead < 4, up_turn, jnp.where(ahead == 4, 0, down_turn)))

    def pass_on(kk, half, j):
        m = j // 2
        rb = 2 * half + j % 2
        k, ahead, stage = column_of(kk)
        heard = (turn_of(ahead, half) > 0) & (ahead != 0)
        upward = (ahead < 4) | ((ahead == 4) & (half == 0))
        last = (ahead == 0) | (ahead == 1) | (ahead == 7)
        owner = base + 4 * k + rb

        @pl.when(heard)
        def _():
            on_copy(kk, rb, m, sib).wait_recv()
        value = (part[kk, rb, m] + recv[kk, rb, m].astype(F32)).astype(BF16)
        send[kk, rb, m] = value

        @pl.when(jnp.logical_not(last))
        def _():
            on_copy(kk, rb, m, jnp.where(upward, chip(z + 2, core), chip(z - 2, core))).start()

        @pl.when(last & (owner != f))
        def _():
            way = jnp.where(ahead == 0, 2, jnp.where(ahead == 1, 0, 1))
            fin_copy(kk, rb, m, way, owner).start()

        @pl.when(last & (owner == f))
        def _():
            fin[2, m] = value

    def pass_turn(kks, turn):
        halves = [(kk, half) for kk in kks for half in (0, 1)]
        due = [turn_of(column_of(kk)[1], half) == turn for kk, half in halves]

        def step(j, carry):
            for (kk, half), now in zip(halves, due):
                @pl.when(now)
                def _():
                    pass_on(kk, half, j)
            return carry

        lax.fori_loop(0, PIECES // 2, step, 0)

    def work(i, carry):
        kk = jnp.where(i == 0, first, 1 - first)
        for q in range(1, 8):
            w2_in = wts.at[kk, (r + q) % 8]
            to_rep(w2_in, w2_in, w2_send.at[kk, q], w2_recv.at[kk, (r + q) % 8], r).wait_recv()
        column(kk)

        pass_turn((kk,), 0)
        return carry

    lax.fori_loop(0, 2, work, 0)

    def pass_rest(turn, carry):
        pass_turn((first, 1 - first), turn)
        return carry

    lax.fori_loop(1, 5, pass_rest, 0)

    c_m = (table[0], table[1])
    ct_m = (table[2], table[3])
    is_middle = (m_own == k_own) & (p_own == k_own % 2) & (core == h_own)
    moments = []
    coeffs = []
    for m in range(3):
        for way in (0, 1):
            fin_copy(0, 0, m, way, sib).wait_recv()

        @pl.when(jnp.logical_not(is_middle))
        def _():
            fin_copy(0, 0, m, 2, sib).wait_recv()
        total = fin[0, m].astype(F32) + fin[1, m].astype(F32) + fin[2, m].astype(F32)
        moment = 0.999 * mom[m] + total
        moments.append(moment)
        inner = mm3(c_m, split(moment), NN)
        coeff_t = mm3(c_m, split(inner), NT)
        coeffs.append(coeff_t)
        hi, lo = split(coeff_t)
        picked = mm(hi, pick_r[m], NN) + mm(lo, pick_r[m], NN)
        band_row = jnp.sum(picked * pick_c[m].astype(F32), axis=0, keepdims=True)
        for q in range(4):
            vals[4 * m + q:4 * m + q + 1, :] = band_row[:, q * SIDE:(q + 1) * SIDE]
    rep_copies = [to_rep(vals, vals_all.at[r], rep_send.at[i], rep_recv.at[r], (r + i) % 8) for i in range(1, 8)]
    for c in rep_copies:
        c.start()
    vals_all[r] = vals[...]

    for m in range(3):
        placed = jnp.where(mask[m] > 0.5, coeffs[m], 0.0)
        half = mm3(ct_m, split(placed), NT)
        out[m] = moments[m] - mm3(split(half), c_m, NN)

    for i in range(1, 8):
        q = (r + i) % 8
        to_rep(vals, vals_all.at[q], rep_send.at[i], rep_recv.at[q], q).wait_recv()
    summed = vals_all[0]
    for i in range(1, 8):
        summed = summed + vals_all[i]
    for m in range(3):
        hi, lo = split(jnp.concatenate([summed[4 * m + q:4 * m + q + 1, :] for q in range(4)], axis=1))
        cols = pick_c[m].astype(F32)
        placed = mm((cols * hi.astype(F32)).astype(BF16), pick_r[m], NT) + mm(
            (cols * lo.astype(F32)).astype(BF16), pick_r[m], NT
        )
        half = mm3(ct_m, split(placed), NT)
        out[3 + m] = mm3(split(half), c_m, NN)

    for c in to_partner + pass_near + pass_far + [to_up, to_down, to_sib, on_sib, near_sib]:
        c.wait_send()
    for c in rep_copies:
        c.wait_send()
    for i, target in enumerate(w1_to[:-1]):
        w1_copy(i, target).wait_send()

    @pl.when(jnp.logical_not(w1_self))
    def _():
        w1_copy(7, w1_to[-1]).wait_send()

    def drain(kk, carry):
        k = column_of(kk)[0]
        for i in range(1, 8):
            w2_copy(kk, i).wait_send()
        for j in range(PIECES):
            @pl.when(base + 4 * k + j % 4 != f)
            def _():
                on_copy(kk, j % 4, j // 4, sib).wait_send()
        return carry

    lax.fori_loop(0, 2, drain, 0)


def write_out(all_ref, *refs):
    outs, sems = refs[:6], refs[6]
    copies = [
        pltpu.make_async_copy(all_ref.at[i], o.at[(0, 0) if i < 3 else (0,)], sems.at[i]) for i, o in enumerate(outs)
    ]
    for c in copies:
        c.start()
    for c in copies:
        c.wait()


def per_device(x_in, d_out, gate_weight, up_weight, down_weight, mom_gate, mom_up, mom_down, band_index):
    dma = pltpu.SemaphoreType.DMA
    block = (SIDE, SIDE)
    scratch = [
        pltpu.VMEM((2, 8 * SIDE, WIDE), BF16),
        pltpu.VMEM((3,) + block, BF16),
        pltpu.VMEM((2, 8, 4, 3, 16, SIDE), BF16),
        pltpu.VMEM((2, 4, 3) + block, F32),
        pltpu.VMEM((2, 4, 3) + block, BF16),
        pltpu.VMEM((2, 4, 3) + block, BF16),
        pltpu.VMEM((3, 3) + block, BF16),
        pltpu.VMEM((3,) + block, F32),
        pltpu.VMEM((3, 1, KEEP), jnp.int32),
        pltpu.VMEM((4,) + block, BF16),
        pltpu.VMEM((3, SIDE, KEEP), BF16),
        pltpu.VMEM((3, SIDE, KEEP), BF16),
        pltpu.VMEM((3,) + block, F32),
        pltpu.VMEM((16, SIDE), F32),
        pltpu.VMEM((8, 16, SIDE), F32),
        dma((10,)),
        dma((17,)),
        dma((17,)),
        dma((8,)),
        dma((2, 4)),
        dma((2, 8)),
        dma((2, 8)),
        dma((2, 4, 3)),
        dma((2, 4, 3)),
        dma((3, 3)),
        dma((8,)),
        dma((8,)),
    ]
    hbm = pl.BlockSpec(memory_space=pltpu.HBM)
    vmem = pl.BlockSpec(memory_space=pltpu.VMEM)
    results = pl.pallas_call(
        kernel,
        out_shape=jax.ShapeDtypeStruct((6,) + block, F32),
        in_specs=[hbm] * 10,
        out_specs=vmem,
        scratch_shapes=scratch,
        compiler_params=pltpu.CompilerParams(
            collective_id=0, has_side_effects=True, vmem_limit_bytes=62 * 1024 * 1024
        ),
        cost_estimate=pl.CostEstimate(flops=1700000000, bytes_accessed=2000000, transcendentals=300000),
    )(
        x_in, d_out, gate_weight, up_weight, down_weight, mom_gate, mom_up, mom_down, band_index,
        jnp.asarray(dct_parts()),
    )
    outs = [jax.ShapeDtypeStruct((1, 1) + block, F32)] * 3 + [jax.ShapeDtypeStruct((1,) + block, F32)] * 3
    return pl.pallas_call(
        write_out, out_shape=outs, in_specs=[vmem], out_specs=[hbm] * 6, scratch_shapes=[dma((6,))]
    )(results)


def solution(mesh):
    tokens = P("rep", "fsdp", None)
    weights = P("fsdp", None, None)
    moments = P("rep", "fsdp", None, None)
    return jax.shard_map(
        per_device, mesh=mesh,
        in_specs=(tokens, tokens, weights, weights, weights, moments, moments, moments, P(None, "fsdp", None)),
        out_specs=(moments, moments, moments, weights, weights, weights),
        check_vma=False,
    )
```
